128 devices in a mesh: expert: 16 (over y_hi, x, core), dp: 8 (over y_lo, z).
Axes of the slice: x: 4, y: 4 (y_hi: 2, y_lo: 2; y = y_hi * 2 + y_lo), z: 4, core: 2. Of those that a mesh axis runs over, the one named last changes fastest.
Arguments:
- tokens: bfloat16 [128, 256, 1280], P(('expert', 'dp')), may hold values from -64 to 64
- slot_params: bfloat16 [128, 1280], replicated, may hold values from -1 to 1
- expert_in: bfloat16 [64, 4608, 1280], P('expert', 'dp'), may hold values from -0.15625 to 0.15625
- expert_out: bfloat16 [64, 4608, 1280], P('expert', 'dp'), may hold values from -0.09375 to 0.09375
- grad_out: bfloat16 [128, 256, 1280], P(('expert', 'dp')), may hold values from -6 to 6
Outputs:
- grad_tokens: bfloat16 [128, 256, 1280], P(('expert', 'dp'))
- grad_params: float32 [128, 1280], replicated
- grad_w_in: bfloat16 [64, 4608, 1280], P('expert', 'dp')
- grad_w_out: bfloat16 [64, 4608, 1280], P('expert', 'dp')
The draws below stay inside these ranges and needn't reach their ends.
All inputs are finite; a program needn't handle non-finite values.
Results may differ from the reference program's by a relative error of at most 0.009.
Values may be sent and summed in bfloat16 or wider, within the bound.
No kernel may reach another device: no remote copies, remote signals or barrier semaphores. Data moves between devices by JAX's collectives and lax.ppermute only.
A program may use at most 128 MiB of HBM per device.

```python
import math
import jax
import jax.numpy as jnp
from jax import lax

D = 1280
M = 256
SLOTS = 2
HID = 4608
EXPERTS = 64
SLOTS_ALL = 128
IMAGES = 128


def slot_table(key):
    table = jax.random.truncated_normal(key, -2.5, 2.5, (SLOTS_ALL, D), jnp.float32)
    return table * (1.0 / math.sqrt(D))


def draw_slot_params(key, part):
    return slot_table(key).astype(jnp.bfloat16)


def draw_tokens(key, part):
    key = jax.random.fold_in(key, 2)
    return jax.random.normal(key, (IMAGES, M, D), jnp.float32).astype(jnp.bfloat16)


def level_of(stream_key, dims, shards, low, high):
    gain, own = 1.0, jax.random.fold_in(stream_key, 6)
    for position, blocks in shards:
        heights = jnp.exp(jax.random.uniform(jax.random.fold_in(own, position), (blocks,), jnp.float32, low / len(shards), high / len(shards)))
        gain = gain * jnp.repeat(heights, dims[position] // blocks).reshape([-1 if axis == position else 1 for axis in range(len(dims))])
    return gain


def scatter_about(rng, shape, scale, most, shards=(), kind=jnp.bfloat16):
    factor_of = level_of(rng, shape, shards, -0.22, 0.18) if shards else 1.0
    result = jax.random.normal(rng, shape, jnp.float32) * scale * factor_of
    return jnp.minimum(jnp.maximum(result, -most), most).astype(kind)


def setup_inputs(seed: int = 0) -> dict:
    key_list = jax.random.split(jax.random.key(seed), 6)
    return {
        "tokens": draw_tokens(jax.random.fold_in(key_list[5], 71), 0),
        "slot_params": draw_slot_params(jax.random.fold_in(key_list[5], 71), 0),
        "expert_in": scatter_about(key_list[2], (EXPERTS, HID, D), D ** -0.5, 0.15625, ((0, 16), (1, 8))),
        "expert_out": scatter_about(key_list[3], (EXPERTS, HID, D), HID ** -0.5, 0.09375, ((0, 16), (1, 8))),
        "grad_out": scatter_about(key_list[4], (IMAGES, M, D), 1.0, 6.0, ((0, 128),)),
    }


inv_root_two = 1.0 / math.sqrt(2.0)
inv_root_tau = 1.0 / math.sqrt(2.0 * math.pi)

def gelu_value(values):
    return 0.5 * values * (1.0 + lax.erf(values * inv_root_two))

def gelu_slope(values):
    return 0.5 * (1.0 + lax.erf(values * inv_root_two)) + values * jnp.exp(-0.5 * values * values) * inv_root_tau

def forward_expert(inputs):
    expert_rows, w_first, w_second = inputs
    hidden = jnp.dot(w_first, expert_rows.T, preferred_element_type=jnp.float32)
    active = gelu_value(hidden).astype(jnp.bfloat16)
    return jnp.dot(active.T, w_second, preferred_element_type=jnp.float32).astype(jnp.bfloat16)

def backward_expert(inputs):
    expert_rows, w_first, w_second, d_rows = inputs
    hidden = jnp.dot(w_first, expert_rows.T, preferred_element_type=jnp.float32)
    active = gelu_value(hidden).astype(jnp.bfloat16)
    d_active = jnp.dot(w_second, d_rows.T, preferred_element_type=jnp.float32)
    g_second = jnp.dot(active, d_rows, preferred_element_type=jnp.float32).astype(jnp.bfloat16)
    d_hidden = (d_active * gelu_slope(hidden)).astype(jnp.bfloat16)
    g_first = jnp.dot(d_hidden, expert_rows, preferred_element_type=jnp.float32).astype(jnp.bfloat16)
    d_input = jnp.dot(d_hidden.T, w_first, preferred_element_type=jnp.float32).astype(jnp.bfloat16)
    return (g_first, g_second, d_input)

def reference(tokens, slot_params, expert_in, expert_out, grad_out):
    wide_tokens = tokens.astype(jnp.float32)
    wide_params = slot_params.astype(jnp.float32)
    logits = jnp.einsum('sd,nmd->nsm', wide_params, wide_tokens)
    p_dispatch = jax.nn.softmax(logits, axis=2)
    p_combine = jax.nn.softmax(logits, axis=1)
    dispatch = p_dispatch.astype(jnp.bfloat16)
    combine = p_combine.astype(jnp.bfloat16)
    slot_in = jnp.einsum('nsm,nmd->snd', dispatch.astype(jnp.float32), wide_tokens).astype(jnp.bfloat16)
    rows_in = slot_in.reshape(EXPERTS, SLOTS * IMAGES, D)
    rows_out = lax.map(forward_expert, (rows_in, expert_in, expert_out))
    slot_out = rows_out.reshape(SLOTS_ALL, IMAGES, D)
    wide_grad = grad_out.astype(jnp.float32)
    d_combine = jnp.einsum('nmd,snd->nsm', wide_grad, slot_out.astype(jnp.float32))
    d_slot_out = jnp.einsum('nsm,nmd->snd', combine.astype(jnp.float32), wide_grad).astype(jnp.bfloat16)
    grad_w_in, grad_w_out, d_rows_in = lax.map(backward_expert, (rows_in, expert_in, expert_out, d_slot_out.reshape(EXPERTS, SLOTS * IMAGES, D)))
    wide_slot_in = d_rows_in.reshape(SLOTS_ALL, IMAGES, D).astype(jnp.float32)
    d_dispatch = jnp.einsum('snd,nmd->nsm', wide_slot_in, wide_tokens)
    d_logits = (p_dispatch * (d_dispatch - lax.optimization_barrier(jnp.sum(p_dispatch * d_dispatch, axis=2, keepdims=True))) + p_combine * (d_combine - lax.optimization_barrier(jnp.sum(p_combine * d_combine, axis=1, keepdims=True)))).astype(jnp.bfloat16)
    wide_logits = d_logits.astype(jnp.float32)
    grad_tokens = (jnp.einsum('nsm,snd->nmd', dispatch.astype(jnp.float32), wide_slot_in) + jnp.einsum('nsm,sd->nmd', wide_logits, wide_params)).astype(jnp.bfloat16)
    grad_params = jnp.einsum('nsm,nmd->sd', wide_logits, wide_tokens)
    return (grad_tokens, grad_params, grad_w_in, grad_w_out)
```

```python
import math

import jax
import jax.numpy as jnp
from jax import lax
from jax.sharding import PartitionSpec as P

SLOTS = 2


inv_root_two = 1.0 / math.sqrt(2.0)
inv_root_tau = 1.0 / math.sqrt(2.0 * math.pi)


def gelu_value(values):
    return 0.5 * values * (1.0 + lax.erf(values * inv_root_two))


def gelu_slope(values):
    return (
        0.5 * (1.0 + lax.erf(values * inv_root_two))
        + values * jnp.exp(-0.5 * values * values) * inv_root_tau
    )


def to_experts(blocks):
    n_group = lax.axis_size("dp")
    resident, n_expert, row_block, feature = blocks.shape
    copies = jnp.broadcast_to(blocks[:, :, None], (resident, n_expert, n_group, row_block, feature))
    copies = copies.reshape(resident, n_expert * n_group * row_block, feature)
    return lax.all_to_all(copies, ("expert", "dp"), split_axis=1, concat_axis=1, tiled=True)


def from_experts(partial_value, n_expert):
    n_group = lax.axis_size("dp")
    resident, total_rows, feature = partial_value.shape
    row_block = total_rows // (n_expert * n_group)
    returned = lax.all_to_all(
        partial_value, ("expert", "dp"), split_axis=1, concat_axis=1, tiled=True
    )
    returned = returned.reshape(resident, n_expert, n_group, row_block, feature)
    return jnp.sum(returned, axis=2, dtype=jnp.float32).astype(jnp.bfloat16)


def sum_over_all(value):
    axes = ("expert", "dp")
    n = lax.axis_size(axes)
    rows, feature = value.shape
    terms = lax.all_to_all(value, axes, split_axis=0, concat_axis=0, tiled=True)
    mine = jnp.sum(terms.reshape(n, rows // n, feature), axis=0)
    copies = jnp.broadcast_to(mine[None], (n, rows // n, feature)).reshape(rows, feature)
    return lax.all_to_all(copies, axes, split_axis=0, concat_axis=0, tiled=True)


def per_device(tokens, slot_params, expert_in, expert_out, grad_out):
    n_expert = lax.axis_size("expert")
    images, length, feature = tokens.shape
    resident = expert_in.shape[0]
    logits = jnp.einsum("sd,nmd->nsm", slot_params, tokens, preferred_element_type=jnp.float32)
    p_dispatch = jax.nn.softmax(logits, axis=2)
    p_combine = jax.nn.softmax(logits, axis=1)
    dispatch = p_dispatch.astype(jnp.bfloat16)
    combine = p_combine.astype(jnp.bfloat16)
    slot_in = jnp.einsum(
        "nsm,nmd->snd", dispatch, tokens, preferred_element_type=jnp.float32
    ).astype(jnp.bfloat16)
    blocks = slot_in.reshape(n_expert, resident, SLOTS * images, feature).transpose(1, 0, 2, 3)
    expert_rows = to_experts(blocks)
    hidden = jnp.einsum("ehd,erd->ehr", expert_in, expert_rows, preferred_element_type=jnp.float32)
    active = gelu_value(hidden).astype(jnp.bfloat16)
    partial_value = jnp.einsum(
        "ehr,ehd->erd", active, expert_out, preferred_element_type=jnp.float32
    ).astype(jnp.bfloat16)
    slot_out = (
        from_experts(partial_value, n_expert).transpose(1, 0, 2, 3).reshape(-1, images, feature)
    )
    d_combine = jnp.einsum("nmd,snd->nsm", grad_out, slot_out, preferred_element_type=jnp.float32)
    d_slot_out = jnp.einsum(
        "nsm,nmd->snd", combine, grad_out, preferred_element_type=jnp.float32
    ).astype(jnp.bfloat16)
    d_blocks = d_slot_out.reshape(n_expert, resident, SLOTS * images, feature).transpose(1, 0, 2, 3)
    d_rows = to_experts(d_blocks)
    d_active = jnp.einsum("ehd,erd->ehr", expert_out, d_rows, preferred_element_type=jnp.float32)
    grad_w_out = jnp.einsum(
        "ehr,erd->ehd", active, d_rows, preferred_element_type=jnp.float32
    ).astype(jnp.bfloat16)
    d_hidden = (d_active * gelu_slope(hidden)).astype(jnp.bfloat16)
    grad_w_in = jnp.einsum(
        "ehr,erd->ehd", d_hidden, expert_rows, preferred_element_type=jnp.float32
    ).astype(jnp.bfloat16)
    d_partial = jnp.einsum(
        "ehr,ehd->erd", d_hidden, expert_in, preferred_element_type=jnp.float32
    ).astype(jnp.bfloat16)
    d_slot_in = from_experts(d_partial, n_expert).transpose(1, 0, 2, 3).reshape(-1, images, feature)
    d_dispatch = jnp.einsum("snd,nmd->nsm", d_slot_in, tokens, preferred_element_type=jnp.float32)
    d_logits = (
        p_dispatch * (d_dispatch - jnp.sum(p_dispatch * d_dispatch, axis=2, keepdims=True))
        + p_combine * (d_combine - jnp.sum(p_combine * d_combine, axis=1, keepdims=True))
    ).astype(jnp.bfloat16)
    grad_tokens = (
        jnp.einsum("nsm,snd->nmd", dispatch, d_slot_in, preferred_element_type=jnp.float32)
        + jnp.einsum("nsm,sd->nmd", d_logits, slot_params, preferred_element_type=jnp.float32)
    ).astype(jnp.bfloat16)
    local_params = jnp.einsum("nsm,nmd->sd", d_logits, tokens, preferred_element_type=jnp.float32)
    grad_params = sum_over_all(local_params)
    return (grad_tokens, grad_params, grad_w_in, grad_w_out)


def solution(mesh):
    placed = (
        P(("expert", "dp"), None, None),
        P(),
        P("expert", "dp", None),
        P("expert", "dp", None),
        P(("expert", "dp"), None, None),
    )
    return jax.shard_map(
        per_device,
        mesh=mesh,
        in_specs=placed,
        out_specs=(
            P(("expert", "dp"), None, None),
            P(),
            P("expert", "dp", None),
            P("expert", "dp", None),
        ),
        check_vma=False,
    )
```

```python
import functools
import math

import jax
import jax.numpy as jnp
from jax import lax
from jax.experimental import pallas as pl
from jax.experimental.pallas import tpu as pltpu
from jax.sharding import Mesh, PartitionSpec as P

SLOTS = 2
NAMES = ("yh", "x", "c", "yl", "z")
EXPERT = ("yh", "x", "c")
GROUP = ("yl", "z")
SWAP = [(0, 1), (1, 0)]
BF = jnp.bfloat16
F32 = jnp.float32

inv_root_two = 1.0 / math.sqrt(2.0)
inv_root_tau = 1.0 / math.sqrt(2.0 * math.pi)


def dot(a, b, ca, cb):
    return lax.dot_general(a, b, (((ca,), (cb,)), ((), ())), preferred_element_type=F32)


def params(limit=24):
    return pltpu.CompilerParams(vmem_limit_bytes=limit * 2**20)


def up(value):
    return lax.ppermute(value, "z", [(i, (i + 1) % 4) for i in range(4)])


def down(value):
    return lax.ppermute(value, "z", [(i, (i + 3) % 4) for i in range(4)])


def across(value):
    return lax.ppermute(value, "yl", SWAP)


def one_hot_rows(rows, n_expert, resident):
    r = lax.broadcasted_iota(jnp.int32, (rows, rows), 0)
    k = lax.broadcasted_iota(jnp.int32, (rows, rows), 1)
    per = n_expert * SLOTS
    e, kind, source, s = r // (2 * per), r // per % 2, r % per // SLOTS, r % SLOTS
    wanted = ((source * 2 + kind) * resident + e) * SLOTS + s
    return (k == wanted).astype(F32).astype(BF)


def route_kernel(n_expert, tokens, slot_params, grad_out, rows, p_dispatch, p_combine):
    t = tokens[0]
    slots, feature = slot_params.shape
    logits = dot(slot_params[...], t, 1, 1)
    wide = jnp.exp(logits - jnp.max(logits, axis=1, keepdims=True))
    pd = wide / jnp.sum(wide, axis=1, keepdims=True)
    p_dispatch[...] = pd
    tall = jnp.exp(logits - jnp.max(logits, axis=0, keepdims=True))
    pc = tall / jnp.sum(tall, axis=0, keepdims=True)
    p_combine[...] = pc
    shape = (n_expert, slots // n_expert, feature)
    slot_in = dot(pd.astype(BF), t, 1, 0).reshape(shape)
    d_slot_out = dot(pc.astype(BF), grad_out[0], 1, 0).reshape(shape)
    both = jnp.concatenate([slot_in, d_slot_out], axis=1).astype(BF)
    rows[...] = both.reshape(rows.shape)


def route(tokens, slot_params, grad_out, n_expert):
    _, length, feature = tokens.shape
    slots = slot_params.shape[0]
    rows = jax.ShapeDtypeStruct((2 * slots, feature), BF)
    probs = jax.ShapeDtypeStruct((slots, length), F32)
    return pl.pallas_call(
        functools.partial(route_kernel, n_expert),
        out_shape=(rows, probs, probs),
        compiler_params=params(),
        name="route",
    )(tokens, slot_params, grad_out)


def sort_kernel(n_expert, resident, rows, whole, first, second):
    n = rows.shape[0]
    out = dot(one_hot_rows(n, n_expert, resident), rows[...], 1, 0).astype(BF)
    whole[...] = out.reshape(whole.shape)
    half = out.reshape(2, *first.shape)
    first[...] = half[0]
    second[...] = half[1]


def sort_rows(rows, n_expert, resident):
    n, feature = rows.shape
    block = n // resident
    return pl.pallas_call(
        functools.partial(sort_kernel, n_expert, resident),
        out_shape=(
            jax.ShapeDtypeStruct((resident, block, feature), BF),
            jax.ShapeDtypeStruct((resident // 2, block, feature), BF),
            jax.ShapeDtypeStruct((resident // 2, block, feature), BF),
        ),
        compiler_params=params(),
        name="sort_rows",
    )(rows)


def after(values, others):
    return lax.optimization_barrier((tuple(values), tuple(others)))[0]


def gather(whole, first, second):
    low_first, high_second = up(first), down(second)
    low_second, high_first = up(second), down(first)
    y = across(whole)
    (y,) = after((y,), (low_second, high_first))
    far_first, far_second = up(low_first), down(high_second)
    y_low, y_high = up(y), down(y)
    y_far_first, y_far_second = across(far_first), across(far_second)
    return (
        first, second, low_first, low_second, far_first, far_second, high_first, high_second,
        y, y_low, y_far_first, y_far_second, y_high,
    )


def piece_specs(block, feature, resident):
    half = resident // 2
    whole = pl.BlockSpec((1, block, feature), lambda e: (e, 0, 0))
    first = pl.BlockSpec((1, block, feature), lambda e: (jnp.minimum(e, half - 1), 0, 0))
    second = pl.BlockSpec((1, block, feature), lambda e: (jnp.maximum(e - half, 0), 0, 0))
    return whole, first, second


def assemble(refs, into, resident):
    e = pl.program_id(0)
    part = refs[0].shape[1] // 2
    halves = {0: (0, 1), 1: (2, 3), 2: (4, 5), 3: (6, 7), 6: (10, 11)}
    wholes = {4: 8, 5: 9, 7: 12}

    def copy(place, ref):
        for kind in range(2):
            into[kind, place * part : (place + 1) * part] = ref[0, kind * part : (kind + 1) * part]

    for place, at in wholes.items():
        copy(place, refs[at])

    @pl.when(e < resident // 2)
    def _():
        for place, (one, _) in halves.items():
            copy(place, refs[one])

    @pl.when(e >= resident // 2)
    def _():
        for place, (_, two) in halves.items():
            copy(place, refs[two])


def scatter_out(kind, total, refs, resident):
    e = pl.program_id(0)
    part = refs[0].shape[1] // 2
    own, y_own, low1, low2, far1, far2, high1, high2, yfar1, yfar2, ylow, yhigh = refs

    def put(ref, place):
        ref[0, kind * part : (kind + 1) * part] = total[place * part : (place + 1) * part]

    put(own, 0)
    put(y_own, 4)
    put(ylow, 5)
    put(yhigh, 7)

    @pl.when(e < resident // 2)
    def _():
        for ref, place in ((low1, 1), (far1, 2), (high1, 3), (yfar1, 6)):
            put(ref, place)

    @pl.when(e >= resident // 2)
    def _():
        for ref, place in ((low2, 1), (far2, 2), (high2, 3), (yfar2, 6)):
            put(ref, place)


def expert_kernel(resident, *refs):
    pieces, (w_in, w_out), (active, d_hidden) = refs[:13], refs[13:15], refs[15:17]
    partial, rows = refs[17:29], refs[29]
    assemble(pieces, rows, resident)
    hidden = dot(w_in[0], rows[0], 1, 1)
    d_active = dot(w_out[0], rows[1], 1, 1)
    bell = 0.5 * (1.0 + lax.erf(hidden * inv_root_two))
    act = (hidden * bell).astype(BF)
    active[0] = act
    slope = bell + hidden * jnp.exp(-0.5 * hidden * hidden) * inv_root_tau
    dh = (d_active * slope).astype(BF)
    d_hidden[0] = dh
    scatter_out(0, dot(act, w_out[0], 0, 0).astype(BF), partial, resident)
    scatter_out(1, dot(dh, w_in[0], 0, 0).astype(BF), partial, resident)


def per_expert(*shape):
    return pl.BlockSpec((1, *shape), lambda e: (e, 0, 0))


def expert_call(pieces, w_in, w_out):
    resident, hid, feature = w_in.shape
    block = pieces[8].shape[1]
    total = 4 * block
    whole, first, second = piece_specs(block, feature, resident)
    halves = [first, second]
    in_specs = halves * 4 + [whole, whole] + halves + [whole]
    in_specs += [per_expert(hid, feature)] * 2
    wide = jax.ShapeDtypeStruct((resident, block, feature), BF)
    half = jax.ShapeDtypeStruct((resident // 2, block, feature), BF)
    out_shape = [jax.ShapeDtypeStruct((resident, hid, total), BF)] * 2
    out_shape += [wide, wide] + [half] * 8 + [wide, wide]
    out_specs = [per_expert(hid, total)] * 2
    out_specs += [whole, whole] + halves * 4 + [whole, whole]
    work = resident * hid * total * feature
    return pl.pallas_call(
        functools.partial(expert_kernel, resident),
        grid=(resident,),
        in_specs=in_specs,
        out_specs=out_specs,
        out_shape=out_shape,
        scratch_shapes=[pltpu.VMEM((2, total, feature), BF)],
        compiler_params=params(60),
        cost_estimate=pl.CostEstimate(flops=8 * work, bytes_accessed=24 * 2**20, transcendentals=0),
        name="expert",
    )(*pieces, w_in, w_out)


def weights_kernel(resident, *refs):
    pieces, (active, d_hidden) = refs[:13], refs[13:15]
    grad_w_out, grad_w_in, rows = refs[15:]
    assemble(pieces, rows, resident)
    grad_w_out[0] = dot(active[0], rows[1], 1, 0).astype(BF)
    grad_w_in[0] = dot(d_hidden[0], rows[0], 1, 0).astype(BF)


def weight_grads(pieces, active, d_hidden):
    resident, hid, total = active.shape
    block, feature = pieces[8].shape[1:]
    whole, first, second = piece_specs(block, feature, resident)
    halves = [first, second]
    in_specs = halves * 4 + [whole, whole] + halves + [whole]
    in_specs += [per_expert(hid, total)] * 2
    out = jax.ShapeDtypeStruct((resident, hid, feature), BF)
    work = resident * hid * total * feature
    return pl.pallas_call(
        functools.partial(weights_kernel, resident),
        grid=(resident,),
        in_specs=in_specs,
        out_specs=[per_expert(hid, feature)] * 2,
        out_shape=[out, out],
        scratch_shapes=[pltpu.VMEM((2, total, feature), BF)],
        compiler_params=params(60),
        cost_estimate=pl.CostEstimate(flops=4 * work, bytes_accessed=20 * 2**20, transcendentals=0),
        name="weight_grads",
    )(*pieces, active, d_hidden)


def add(*values):
    return sum(v.astype(F32) for v in values).astype(BF)


def reduce_back(parts, between):
    own, y_own, low1, low2, far1, far2, high1, high2, yfar1, yfar2, ylow, yhigh = parts
    w1, w2 = across(yfar1), across(yfar2)
    v_up, v_down = up(yhigh), down(ylow)
    w1, w2 = after((w1, w2), between)
    high2, low1 = after((high2, low1), (w1, w2))
    s_up2, s_down1 = up(high2), down(low1)
    h1, h2 = up(add(far1, w1)), down(add(far2, w2))
    wy = across(add(y_own, v_up, v_down))
    s_up1, s_down2 = up(add(high1, h1)), down(add(low2, h2))
    return own, wy, s_up1, s_up2, s_down1, s_down2


def unsort_kernel(n_expert, own, wy, up1, up2, down1, down2, out):
    resident, block, feature = own.shape
    half = resident // 2
    n = resident * block
    wide = lambda ref: ref[...].astype(F32)
    base = wide(own) + wide(wy)
    first = base[:half] + wide(up1) + wide(down1)
    second = base[half:] + wide(up2) + wide(down2)
    total = jnp.concatenate([first, second], axis=0).reshape(n, feature).astype(BF)
    out[...] = dot(one_hot_rows(n, n_expert, resident), total, 0, 0).astype(BF)


def unsort_rows(pieces, n_expert):
    resident, block, feature = pieces[0].shape
    return pl.pallas_call(
        functools.partial(unsort_kernel, n_expert),
        out_shape=jax.ShapeDtypeStruct((resident * block, feature), BF),
        compiler_params=params(),
        name="unsort_rows",
    )(*pieces)


def exchange(rows):
    return lax.all_to_all(rows, EXPERT, split_axis=0, concat_axis=0, tiled=True)


def logits_kernel(n_expert, tokens, grad_out, back, p_dispatch, p_combine, d_logits, local, d_slot):
    t = tokens[0]
    n, feature = back.shape
    wide = back[...].astype(F32).reshape(n_expert, n // n_expert, feature)
    split = n // n_expert // 2
    slot_out = wide[:, :split].reshape(n // 2, feature).astype(BF)
    d_slot_in = wide[:, split:].reshape(n // 2, feature).astype(BF)
    d_slot[...] = d_slot_in
    d_combine = dot(slot_out, grad_out[0], 1, 1)
    d_dispatch = dot(d_slot_in, t, 1, 1)
    pd, pc = p_dispatch[...], p_combine[...]
    grad = pd * (d_dispatch - jnp.sum(pd * d_dispatch, axis=1, keepdims=True)) + pc * (
        d_combine - jnp.sum(pc * d_combine, axis=0, keepdims=True)
    )
    dl = grad.astype(BF)
    d_logits[...] = dl
    local[...] = dot(dl, t, 1, 0)


def logits_back(tokens, grad_out, back, p_dispatch, p_combine, n_expert):
    slots = p_dispatch.shape[0]
    feature = back.shape[1]
    return pl.pallas_call(
        functools.partial(logits_kernel, n_expert),
        out_shape=(
            jax.ShapeDtypeStruct(p_dispatch.shape, BF),
            jax.ShapeDtypeStruct((slots, feature), F32),
            jax.ShapeDtypeStruct((slots, feature), BF),
        ),
        compiler_params=params(),
        name="logits_back",
    )(tokens, grad_out, back, p_dispatch, p_combine)


def tokens_kernel(p_dispatch, d_slot_in, d_logits, slot_params, grad_tokens):
    first = dot(p_dispatch[...].astype(BF), d_slot_in[...], 0, 0)
    second = dot(d_logits[...], slot_params[...], 0, 0)
    grad_tokens[0] = (first + second).astype(BF)


def tokens_back(p_dispatch, d_slot_in, d_logits, slot_params):
    slots, length = p_dispatch.shape
    feature = slot_params.shape[1]
    return pl.pallas_call(
        tokens_kernel,
        out_shape=jax.ShapeDtypeStruct((1, length, feature), BF),
        compiler_params=params(),
        name="tokens_back",
    )(p_dispatch, d_slot_in, d_logits, slot_params)


def sum_over_all(value):
    n = lax.axis_size(NAMES)
    rows, feature = value.shape
    terms = lax.all_to_all(value, NAMES, split_axis=0, concat_axis=0, tiled=True)
    mine = jnp.sum(terms.reshape(n, rows // n, feature), axis=0)
    copies = jnp.broadcast_to(mine[None], (n, rows // n, feature)).reshape(rows, feature)
    return lax.all_to_all(copies, NAMES, split_axis=0, concat_axis=0, tiled=True)


def per_device(tokens, slot_params, expert_in, expert_out, grad_out):
    n_expert = lax.axis_size(EXPERT)
    resident = expert_in.shape[0]
    outgoing, p_dispatch, p_combine = route(tokens, slot_params, grad_out, n_expert)
    pieces = gather(*sort_rows(exchange(outgoing), n_expert, resident))
    active, d_hidden, *partial = expert_call(pieces, expert_in, expert_out)
    grad_w_out, grad_w_in = weight_grads(pieces, active, d_hidden)
    sums = reduce_back(partial, (grad_w_out, grad_w_in))
    back = exchange(unsort_rows(sums, n_expert))
    d_logits, local_params, d_slot_in = logits_back(
        tokens, grad_out, back, p_dispatch, p_combine, n_expert
    )
    grad_params = sum_over_all(local_params)
    grad_tokens = tokens_back(p_dispatch, d_slot_in, d_logits, slot_params)
    return (grad_tokens, grad_params, grad_w_in, grad_w_out)


def solution(mesh):
    parts = Mesh(mesh.devices.reshape(2, 4, 2, 2, 4), NAMES)
    image = P(NAMES, None, None)
    weight = P(EXPERT, GROUP, None)
    return jax.shard_map(
        per_device,
        mesh=parts,
        in_specs=(image, P(), weight, weight, image),
        out_specs=(image, P(), weight, weight),
        check_vma=False,
    )
```

```python
import functools
import math

import jax
import jax.numpy as jnp
from jax import lax
from jax.experimental import pallas as pl
from jax.experimental.pallas import tpu as pltpu
from jax.sharding import Mesh, PartitionSpec as P

SLOTS = 2
NAMES = ("yh", "x", "c", "yl", "z")
EXPERT = ("yh", "x", "c")
GROUP = ("yl", "z")
SWAP = [(0, 1), (1, 0)]
BF = jnp.bfloat16
F32 = jnp.float32

inv_root_two = 1.0 / math.sqrt(2.0)
inv_root_tau = 1.0 / math.sqrt(2.0 * math.pi)


def dot(a, b, ca, cb):
    return lax.dot_general(a, b, (((ca,), (cb,)), ((), ())), preferred_element_type=F32)


def params(limit=24):
    return pltpu.CompilerParams(vmem_limit_bytes=limit * 2**20)


def up(value, name):
    with jax.named_scope(name + "_up"):
        return lax.ppermute(value, "z", [(i, (i + 1) % 4) for i in range(4)])


def down(value, name):
    with jax.named_scope(name + "_down"):
        return lax.ppermute(value, "z", [(i, (i + 3) % 4) for i in range(4)])


def across(value, name):
    with jax.named_scope(name + "_across"):
        return lax.ppermute(value, "yl", SWAP)


def one_hot_rows(rows, n_expert, resident):
    r = lax.broadcasted_iota(jnp.int32, (rows, rows), 0)
    k = lax.broadcasted_iota(jnp.int32, (rows, rows), 1)
    per = n_expert * SLOTS
    e, kind, source, s = r // (2 * per), r // per % 2, r % per // SLOTS, r % SLOTS
    wanted = ((source * 2 + kind) * resident + e) * SLOTS + s
    return (k == wanted).astype(F32).astype(BF)


def route_kernel(n_expert, tokens, slot_params, grad_out, rows, p_dispatch, p_combine):
    t = tokens[0]
    slots, feature = slot_params.shape
    logits = dot(slot_params[...], t, 1, 1)
    wide = jnp.exp(logits - jnp.max(logits, axis=1, keepdims=True))
    pd = wide / jnp.sum(wide, axis=1, keepdims=True)
    p_dispatch[...] = pd
    tall = jnp.exp(logits - jnp.max(logits, axis=0, keepdims=True))
    pc = tall / jnp.sum(tall, axis=0, keepdims=True)
    p_combine[...] = pc
    shape = (n_expert, slots // n_expert, feature)
    slot_in = dot(pd.astype(BF), t, 1, 0).reshape(shape)
    d_slot_out = dot(pc.astype(BF), grad_out[0], 1, 0).reshape(shape)
    both = jnp.concatenate([slot_in, d_slot_out], axis=1).astype(BF)
    rows[...] = both.reshape(rows.shape)


def route(tokens, slot_params, grad_out, n_expert):
    _, length, feature = tokens.shape
    slots = slot_params.shape[0]
    rows = jax.ShapeDtypeStruct((2 * slots, feature), BF)
    probs = jax.ShapeDtypeStruct((slots, length), F32)
    return pl.pallas_call(
        functools.partial(route_kernel, n_expert),
        out_shape=(rows, probs, probs),
        compiler_params=params(60),
        name="route",
    )(tokens, slot_params, grad_out)


def sort_kernel(n_expert, resident, rows, first, second):
    n = rows.shape[0]
    out = dot(one_hot_rows(n, n_expert, resident), rows[...], 1, 0).astype(BF)
    half = out.reshape(2, *first.shape)
    first[...] = half[0]
    second[...] = half[1]


def sort_rows(rows, n_expert, resident):
    n, feature = rows.shape
    half = jax.ShapeDtypeStruct((resident // 2, n // resident, feature), BF)
    return pl.pallas_call(
        functools.partial(sort_kernel, n_expert, resident),
        out_shape=(half, half),
        compiler_params=params(),
        name="sort_rows",
    )(rows)


def after(values, others):
    return lax.optimization_barrier((tuple(values), tuple(others)))[0]


def gather(first, second):
    low1, high1, y1 = up(first, "first"), down(first, "first"), across(first, "first")
    low2, high2, y2 = up(second, "second"), down(second, "second"), across(second, "second")
    far1, far2 = up(low1, "first_on"), down(high2, "second_on")
    y_low1, y_high1 = up(y1, "first_y"), down(y1, "first_y")
    one = (first, low1, far1, high1, y1, y_low1, across(far1, "first_far"), y_high1)
    (y2,) = after((y2,), (far1,))
    y_low2, y_high2 = up(y2, "second_y"), down(y2, "second_y")
    two = (second, low2, far2, high2, y2, y_low2, across(far2, "second_far"), y_high2)
    return one, two


def assemble(refs, into):
    part = refs[0].shape[1] // 2
    for place, ref in enumerate(refs):
        for kind in range(2):
            into[kind, place * part : (place + 1) * part] = ref[0, kind * part : (kind + 1) * part]


def scatter_out(kind, total, refs):
    part = refs[0].shape[1] // 2
    for place, ref in enumerate(refs):
        ref[0, kind * part : (kind + 1) * part] = total[place * part : (place + 1) * part]


def expert_kernel(*refs):
    pieces, (w_in, w_out), (active, d_hidden) = refs[:8], refs[8:10], refs[10:12]
    partial, rows = refs[12:20], refs[20]
    assemble(pieces, rows)
    hidden = dot(w_in[0], rows[0], 1, 1)
    d_active = dot(w_out[0], rows[1], 1, 1)
    bell = 0.5 * (1.0 + lax.erf(hidden * inv_root_two))
    act = (hidden * bell).astype(BF)
    active[0] = act
    slope = bell + hidden * jnp.exp(-0.5 * hidden * hidden) * inv_root_tau
    dh = (d_active * slope).astype(BF)
    d_hidden[0] = dh
    scatter_out(0, dot(act, w_out[0], 0, 0).astype(BF), partial)
    scatter_out(1, dot(dh, w_in[0], 0, 0).astype(BF), partial)


def per_expert(*shape, base=0):
    return pl.BlockSpec((1, *shape), lambda e: (e + base, 0, 0))


def expert_call(pieces, w_in, w_out, base):
    _, hid, feature = w_in.shape
    count, block, _ = pieces[0].shape
    total = 4 * block
    work = count * hid * total * feature
    return pl.pallas_call(
        expert_kernel,
        grid=(count,),
        in_specs=[per_expert(block, feature)] * 8 + [per_expert(hid, feature, base=base)] * 2,
        out_specs=[per_expert(hid, total)] * 2 + [per_expert(block, feature)] * 8,
        out_shape=[jax.ShapeDtypeStruct((count, hid, total), BF)] * 2
        + [jax.ShapeDtypeStruct((count, block, feature), BF)] * 8,
        scratch_shapes=[pltpu.VMEM((2, total, feature), BF)],
        compiler_params=params(60),
        cost_estimate=pl.CostEstimate(flops=8 * work, bytes_accessed=12 * 2**20, transcendentals=0),
        name="expert",
    )(*pieces, w_in, w_out)


def weights_kernel(half, *refs):
    one, two = refs[:10], refs[10:20]
    grad_w_out, grad_w_in, rows = refs[20:]

    def work(pieces, active, d_hidden):
        assemble(pieces, rows)
        grad_w_out[0] = dot(active[0], rows[1], 1, 0).astype(BF)
        grad_w_in[0] = dot(d_hidden[0], rows[0], 1, 0).astype(BF)

    @pl.when(pl.program_id(0) < half)
    def _():
        work(one[:8], *one[8:])

    @pl.when(pl.program_id(0) >= half)
    def _():
        work(two[:8], *two[8:])


def weight_grads(one, two):
    half, hid, total = one[8].shape
    block, feature = one[0].shape[1:]

    def first(*shape):
        return pl.BlockSpec((1, *shape), lambda e: (jnp.minimum(e, half - 1), 0, 0))

    def second(*shape):
        return pl.BlockSpec((1, *shape), lambda e: (jnp.maximum(e - half, 0), 0, 0))

    in_specs = []
    for spec in (first, second):
        in_specs += [spec(block, feature)] * 8 + [spec(hid, total)] * 2
    out = jax.ShapeDtypeStruct((2 * half, hid, feature), BF)
    work = 2 * half * hid * total * feature
    return pl.pallas_call(
        functools.partial(weights_kernel, half),
        grid=(2 * half,),
        in_specs=in_specs,
        out_specs=[per_expert(hid, feature)] * 2,
        out_shape=[out, out],
        scratch_shapes=[pltpu.VMEM((2, total, feature), BF)],
        compiler_params=params(60),
        cost_estimate=pl.CostEstimate(flops=4 * work, bytes_accessed=20 * 2**20, transcendentals=0),
        name="weight_grads",
    )(*one, *two)


def add(*values):
    return sum(v.astype(F32) for v in values).astype(BF)


def reduce(parts, far_way, name):
    own, low, far, high, y, y_low, y_far, y_high = parts
    w = across(y_far, name + "_far")
    v_up, v_down = up(y_high, name + "_y"), down(y_low, name + "_y")
    near, last, other_way = (low, high, down) if far_way is up else (high, low, up)
    direct = other_way(near, name)
    chain = far_way(add(last, far_way(add(far, w), name + "_on")), name)
    return own, direct, chain, across(add(y, v_up, v_down), name)


def unsort_kernel(n_expert, n_first, *refs):
    out = refs[-1]
    half, block, feature = refs[0].shape
    n = 2 * half * block
    first = sum(ref[...].astype(F32) for ref in refs[:n_first])
    second = sum(ref[...].astype(F32) for ref in refs[n_first:-1])
    total = jnp.concatenate([first, second], axis=0).reshape(n, feature).astype(BF)
    out[...] = dot(one_hot_rows(n, n_expert, 2 * half), total, 0, 0).astype(BF)


def unsort_rows(first, second, n_expert):
    half, block, feature = first[0].shape
    return pl.pallas_call(
        functools.partial(unsort_kernel, n_expert, len(first)),
        out_shape=jax.ShapeDtypeStruct((2 * half * block, feature), BF),
        compiler_params=params(),
        name="unsort_rows",
    )(*first, *second)


def exchange(rows):
    return lax.all_to_all(rows, EXPERT, split_axis=0, concat_axis=0, tiled=True)


def logits_kernel(n_expert, tokens, grad_out, back, p_dispatch, p_combine, d_logits, local, d_slot):
    t = tokens[0]
    n, feature = back.shape
    wide = back[...].astype(F32).reshape(n_expert, n // n_expert, feature)
    split = n // n_expert // 2
    slot_out = wide[:, :split].reshape(n // 2, feature).astype(BF)
    d_slot_in = wide[:, split:].reshape(n // 2, feature).astype(BF)
    d_slot[...] = d_slot_in
    d_combine = dot(slot_out, grad_out[0], 1, 1)
    d_dispatch = dot(d_slot_in, t, 1, 1)
    pd, pc = p_dispatch[...], p_combine[...]
    grad = pd * (d_dispatch - jnp.sum(pd * d_dispatch, axis=1, keepdims=True)) + pc * (
        d_combine - jnp.sum(pc * d_combine, axis=0, keepdims=True)
    )
    dl = grad.astype(BF)
    d_logits[...] = dl
    local[...] = dot(dl, t, 1, 0)


def logits_back(tokens, grad_out, back, p_dispatch, p_combine, n_expert):
    slots = p_dispatch.shape[0]
    feature = back.shape[1]
    return pl.pallas_call(
        functools.partial(logits_kernel, n_expert),
        out_shape=(
            jax.ShapeDtypeStruct(p_dispatch.shape, BF),
            jax.ShapeDtypeStruct((slots, feature), F32),
            jax.ShapeDtypeStruct((slots, feature), BF),
        ),
        compiler_params=params(),
        name="logits_back",
    )(tokens, grad_out, back, p_dispatch, p_combine)


def tokens_kernel(p_dispatch, d_slot_in, d_logits, slot_params, grad_tokens):
    first = dot(p_dispatch[...].astype(BF), d_slot_in[...], 0, 0)
    second = dot(d_logits[...], slot_params[...], 0, 0)
    grad_tokens[0] = (first + second).astype(BF)


def tokens_back(p_dispatch, d_slot_in, d_logits, slot_params):
    slots, length = p_dispatch.shape
    feature = slot_params.shape[1]
    return pl.pallas_call(
        tokens_kernel,
        out_shape=jax.ShapeDtypeStruct((1, length, feature), BF),
        compiler_params=params(),
        name="tokens_back",
    )(p_dispatch, d_slot_in, d_logits, slot_params)


def sum_over_all(value):
    n = lax.axis_size(NAMES)
    rows, feature = value.shape
    terms = lax.all_to_all(value, NAMES, split_axis=0, concat_axis=0, tiled=True)
    mine = jnp.sum(terms.reshape(n, rows // n, feature), axis=0)
    copies = jnp.broadcast_to(mine[None], (n, rows // n, feature)).reshape(rows, feature)
    return lax.all_to_all(copies, NAMES, split_axis=0, concat_axis=0, tiled=True)


def split(outputs):
    return outputs[:2], outputs[2:]


def per_device(tokens, slot_params, expert_in, expert_out, grad_out):
    n_expert = lax.axis_size(EXPERT)
    resident = expert_in.shape[0]
    outgoing, p_dispatch, p_combine = route(tokens, slot_params, grad_out, n_expert)
    first, second = sort_rows(exchange(outgoing), n_expert, resident)
    one, two = gather(first, second)
    kept_one, partial_one = split(expert_call(one, expert_in, expert_out, 0))
    sums_one = reduce(partial_one, up, "sum_first")
    kept_two, partial_two = split(expert_call(two, expert_in, expert_out, resident // 2))
    sums_two = reduce(partial_two, down, "sum_second")
    grad_w_out, grad_w_in = weight_grads((*one, *kept_one), (*two, *kept_two))
    back = exchange(unsort_rows(sums_one, sums_two, n_expert))
    d_logits, local_params, d_slot_in = logits_back(
        tokens, grad_out, back, p_dispatch, p_combine, n_expert
    )
    grad_params = sum_over_all(local_params)
    grad_tokens = tokens_back(p_dispatch, d_slot_in, d_logits, slot_params)
    return (grad_tokens, grad_params, grad_w_in, grad_w_out)


def solution(mesh):
    parts = Mesh(mesh.devices.reshape(2, 4, 2, 2, 4), NAMES)
    image = P(NAMES, None, None)
    weight = P(EXPERT, GROUP, None)
    return jax.shard_map(
        per_device,
        mesh=parts,
        in_specs=(image, P(), weight, weight, image),
        out_specs=(image, P(), weight, weight),
        check_vma=False,
    )
```

```python
import functools
import math

import jax
import jax.numpy as jnp
from jax import lax
from jax.experimental import pallas as pl
from jax.experimental.pallas import tpu as pltpu
from jax.sharding import Mesh, PartitionSpec as P

SLOTS = 2
NAMES = ("yh", "x", "c", "yl", "z")
EXPERT = ("yh", "x", "c")
GROUP = ("yl", "z")
SWAP = [(0, 1), (1, 0)]
BF = jnp.bfloat16
F32 = jnp.float32

inv_root_two = 1.0 / math.sqrt(2.0)
inv_root_tau = 1.0 / math.sqrt(2.0 * math.pi)


def dot(a, b, ca, cb):
    return lax.dot_general(a, b, (((ca,), (cb,)), ((), ())), preferred_element_type=F32)


def params(limit=24):
    return pltpu.CompilerParams(vmem_limit_bytes=limit * 2**20)


def up(value, name):
    with jax.named_scope(name + "_up"):
        return lax.ppermute(value, "z", [(i, (i + 1) % 4) for i in range(4)])


def down(value, name):
    with jax.named_scope(name + "_down"):
        return lax.ppermute(value, "z", [(i, (i + 3) % 4) for i in range(4)])


def across(value, name):
    with jax.named_scope(name + "_across"):
        return lax.ppermute(value, "yl", SWAP)


def one_hot_rows(rows, n_expert, resident):
    r = lax.broadcasted_iota(jnp.int32, (rows, rows), 0)
    k = lax.broadcasted_iota(jnp.int32, (rows, rows), 1)
    per = n_expert * SLOTS
    e, kind, source, s = r // (2 * per), r // per % 2, r % per // SLOTS, r % SLOTS
    wanted = ((source * 2 + kind) * resident + e) * SLOTS + s
    return (k == wanted).astype(F32).astype(BF)


def route_kernel(n_expert, tokens, slot_params, grad_out, rows, p_dispatch, p_combine):
    t = tokens[0]
    slots, feature = slot_params.shape
    logits = dot(slot_params[...], t, 1, 1)
    wide = jnp.exp(logits - jnp.max(logits, axis=1, keepdims=True))
    pd = wide / jnp.sum(wide, axis=1, keepdims=True)
    p_dispatch[...] = pd
    tall = jnp.exp(logits - jnp.max(logits, axis=0, keepdims=True))
    pc = tall / jnp.sum(tall, axis=0, keepdims=True)
    p_combine[...] = pc
    shape = (n_expert, slots // n_expert, feature)
    slot_in = dot(pd.astype(BF), t, 1, 0).reshape(shape)
    d_slot_out = dot(pc.astype(BF), grad_out[0], 1, 0).reshape(shape)
    both = jnp.concatenate([slot_in, d_slot_out], axis=1).astype(BF)
    rows[...] = both.reshape(rows.shape)


def route(tokens, slot_params, grad_out, n_expert):
    _, length, feature = tokens.shape
    slots = slot_params.shape[0]
    rows = jax.ShapeDtypeStruct((2 * slots, feature), BF)
    probs = jax.ShapeDtypeStruct((slots, length), F32)
    return pl.pallas_call(
        functools.partial(route_kernel, n_expert),
        out_shape=(rows, probs, probs),
        compiler_params=params(60),
        name="route",
    )(tokens, slot_params, grad_out)


def sort_kernel(n_expert, resident, rows, first, second):
    n = rows.shape[0]
    out = dot(one_hot_rows(n, n_expert, resident), rows[...], 1, 0).astype(BF)
    half = out.reshape(2, *first.shape)
    first[...] = half[0]
    second[...] = half[1]


def sort_rows(rows, n_expert, resident):
    n, feature = rows.shape
    half = jax.ShapeDtypeStruct((resident // 2, n // resident, feature), BF)
    return pl.pallas_call(
        functools.partial(sort_kernel, n_expert, resident),
        out_shape=(half, half),
        compiler_params=params(),
        name="sort_rows",
    )(rows)


def after(values, others):
    return lax.optimization_barrier((tuple(values), tuple(others)))[0]


def stage_kernel(w_in, w_out, near_in, near_out, sems):
    copies = [
        pltpu.make_async_copy(w_in, near_in, sems.at[0]),
        pltpu.make_async_copy(w_out, near_out, sems.at[1]),
    ]
    for copy in copies:
        copy.start()
    for copy in copies:
        copy.wait()


def stage(w_in, w_out):
    return pl.pallas_call(
        stage_kernel,
        in_specs=[pl.BlockSpec(memory_space=pltpu.HBM)] * 2,
        out_specs=[pl.BlockSpec(memory_space=pl.ANY)] * 2,
        out_shape=[jax.ShapeDtypeStruct(w.shape, w.dtype) for w in (w_in, w_out)],
        scratch_shapes=[pltpu.SemaphoreType.DMA((2,))],
        compiler_params=params(40),
        name="stage",
    )(w_in, w_out)


def gather(first, second, w_in, w_out):
    low1, high1, y1 = up(first, "first"), down(first, "first"), across(first, "first")
    low2, high2, y2 = up(second, "second"), down(second, "second"), across(second, "second")
    far1, far2 = up(low1, "first_on"), down(high2, "second_on")
    weights = stage(*after((w_in, w_out), (low1,)))
    y_low1, y_high1 = up(y1, "first_y"), down(y1, "first_y")
    (sent,) = after((far1,), weights)
    one = (first, low1, far1, high1, y1, y_low1, across(sent, "first_far"), y_high1)
    (y2,) = after((y2,), (far1,))
    y_low2, y_high2 = up(y2, "second_y"), down(y2, "second_y")
    two = (second, low2, far2, high2, y2, y_low2, across(far2, "second_far"), y_high2)
    return one, two, weights


def assemble(refs, into):
    part = refs[0].shape[1] // 2
    for place, ref in enumerate(refs):
        for kind in range(2):
            into[kind, place * part : (place + 1) * part] = ref[0, kind * part : (kind + 1) * part]


def scatter_out(kind, total, refs):
    part = refs[0].shape[1] // 2
    for place, ref in enumerate(refs):
        ref[0, kind * part : (kind + 1) * part] = total[place * part : (place + 1) * part]


def expert_kernel(*refs):
    pieces, (w_in, w_out), (active, d_hidden) = refs[:8], refs[8:10], refs[10:12]
    partial, rows = refs[12:20], refs[20]
    assemble(pieces, rows)
    hidden = dot(w_in[0], rows[0], 1, 1)
    d_active = dot(w_out[0], rows[1], 1, 1)
    bell = 0.5 * (1.0 + lax.erf(hidden * inv_root_two))
    act = (hidden * bell).astype(BF)
    active[0] = act
    slope = bell + hidden * jnp.exp(-0.5 * hidden * hidden) * inv_root_tau
    dh = (d_active * slope).astype(BF)
    d_hidden[0] = dh
    scatter_out(0, dot(act, w_out[0], 0, 0).astype(BF), partial)
    scatter_out(1, dot(dh, w_in[0], 0, 0).astype(BF), partial)


def per_expert(*shape, base=0):
    return pl.BlockSpec((1, *shape), lambda e: (e + base, 0, 0))


def expert_call(pieces, w_in, w_out, base):
    _, hid, feature = w_in.shape
    count, block, _ = pieces[0].shape
    total = 4 * block
    work = count * hid * total * feature
    return pl.pallas_call(
        expert_kernel,
        grid=(count,),
        in_specs=[per_expert(block, feature)] * 8 + [per_expert(hid, feature, base=base)] * 2,
        out_specs=[per_expert(hid, total)] * 2 + [per_expert(block, feature)] * 8,
        out_shape=[jax.ShapeDtypeStruct((count, hid, total), BF)] * 2
        + [jax.ShapeDtypeStruct((count, block, feature), BF)] * 8,
        scratch_shapes=[pltpu.VMEM((2, total, feature), BF)],
        compiler_params=params(24),
        cost_estimate=pl.CostEstimate(flops=8 * work, bytes_accessed=12 * 2**20, transcendentals=0),
        name="expert",
    )(*pieces, w_in, w_out)


def weights_kernel(half, *refs):
    one, two = refs[:10], refs[10:20]
    grad_w_out, grad_w_in, rows = refs[20:]

    def work(pieces, active, d_hidden):
        assemble(pieces, rows)
        grad_w_out[0] = dot(active[0], rows[1], 1, 0).astype(BF)
        grad_w_in[0] = dot(d_hidden[0], rows[0], 1, 0).astype(BF)

    @pl.when(pl.program_id(0) < half)
    def _():
        work(one[:8], *one[8:])

    @pl.when(pl.program_id(0) >= half)
    def _():
        work(two[:8], *two[8:])


def weight_grads(one, two):
    half, hid, total = one[8].shape
    block, feature = one[0].shape[1:]

    def first(*shape):
        return pl.BlockSpec((1, *shape), lambda e: (jnp.minimum(e, half - 1), 0, 0))

    def second(*shape):
        return pl.BlockSpec((1, *shape), lambda e: (jnp.maximum(e - half, 0), 0, 0))

    in_specs = []
    for spec in (first, second):
        in_specs += [spec(block, feature)] * 8 + [spec(hid, total)] * 2
    out = jax.ShapeDtypeStruct((2 * half, hid, feature), BF)
    work = 2 * half * hid * total * feature
    return pl.pallas_call(
        functools.partial(weights_kernel, half),
        grid=(2 * half,),
        in_specs=in_specs,
        out_specs=[per_expert(hid, feature)] * 2,
        out_shape=[out, out],
        scratch_shapes=[pltpu.VMEM((2, total, feature), BF)],
        compiler_params=params(60),
        cost_estimate=pl.CostEstimate(flops=4 * work, bytes_accessed=20 * 2**20, transcendentals=0),
        name="weight_grads",
    )(*one, *two)


def add(*values):
    return sum(v.astype(F32) for v in values).astype(BF)


def reduce(parts, far_way, name):
    own, low, far, high, y, y_low, y_far, y_high = parts
    w = across(y_far, name + "_far")
    v_up, v_down = up(y_high, name + "_y"), down(y_low, name + "_y")
    near, last, other_way = (low, high, down) if far_way is up else (high, low, up)
    direct = other_way(near, name)
    chain = far_way(add(last, far_way(add(far, w), name + "_on")), name)
    return own, direct, chain, across(add(y, v_up, v_down), name)


def unsort_kernel(n_expert, n_first, *refs):
    out = refs[-1]
    half, block, feature = refs[0].shape
    n = 2 * half * block
    first = sum(ref[...].astype(F32) for ref in refs[:n_first])
    second = sum(ref[...].astype(F32) for ref in refs[n_first:-1])
    total = jnp.concatenate([first, second], axis=0).reshape(n, feature).astype(BF)
    out[...] = dot(one_hot_rows(n, n_expert, 2 * half), total, 0, 0).astype(BF)


def unsort_rows(first, second, n_expert):
    half, block, feature = first[0].shape
    return pl.pallas_call(
        functools.partial(unsort_kernel, n_expert, len(first)),
        out_shape=jax.ShapeDtypeStruct((2 * half * block, feature), BF),
        compiler_params=params(),
        name="unsort_rows",
    )(*first, *second)


def exchange(rows):
    return lax.all_to_all(rows, EXPERT, split_axis=0, concat_axis=0, tiled=True)


def logits_kernel(n_expert, tokens, grad_out, back, p_dispatch, p_combine, d_logits, local, d_slot):
    t = tokens[0]
    n, feature = back.shape
    wide = back[...].astype(F32).reshape(n_expert, n // n_expert, feature)
    split = n // n_expert // 2
    slot_out = wide[:, :split].reshape(n // 2, feature).astype(BF)
    d_slot_in = wide[:, split:].reshape(n // 2, feature).astype(BF)
    d_slot[...] = d_slot_in
    d_combine = dot(slot_out, grad_out[0], 1, 1)
    d_dispatch = dot(d_slot_in, t, 1, 1)
    pd, pc = p_dispatch[...], p_combine[...]
    grad = pd * (d_dispatch - jnp.sum(pd * d_dispatch, axis=1, keepdims=True)) + pc * (
        d_combine - jnp.sum(pc * d_combine, axis=0, keepdims=True)
    )
    dl = grad.astype(BF)
    d_logits[...] = dl
    local[...] = dot(dl, t, 1, 0)


def logits_back(tokens, grad_out, back, p_dispatch, p_combine, n_expert):
    slots = p_dispatch.shape[0]
    feature = back.shape[1]
    return pl.pallas_call(
        functools.partial(logits_kernel, n_expert),
        out_shape=(
            jax.ShapeDtypeStruct(p_dispatch.shape, BF),
            jax.ShapeDtypeStruct((slots, feature), F32),
            jax.ShapeDtypeStruct((slots, feature), BF),
        ),
        compiler_params=params(),
        name="logits_back",
    )(tokens, grad_out, back, p_dispatch, p_combine)


def tokens_kernel(p_dispatch, d_slot_in, d_logits, slot_params, grad_tokens):
    first = dot(p_dispatch[...].astype(BF), d_slot_in[...], 0, 0)
    second = dot(d_logits[...], slot_params[...], 0, 0)
    grad_tokens[0] = (first + second).astype(BF)


def tokens_back(p_dispatch, d_slot_in, d_logits, slot_params):
    slots, length = p_dispatch.shape
    feature = slot_params.shape[1]
    return pl.pallas_call(
        tokens_kernel,
        out_shape=jax.ShapeDtypeStruct((1, length, feature), BF),
        compiler_params=params(),
        name="tokens_back",
    )(p_dispatch, d_slot_in, d_logits, slot_params)


def sum_over_all(value):
    n = lax.axis_size(NAMES)
    rows, feature = value.shape
    terms = lax.all_to_all(value, NAMES, split_axis=0, concat_axis=0, tiled=True)
    mine = jnp.sum(terms.reshape(n, rows // n, feature), axis=0)
    copies = jnp.broadcast_to(mine[None], (n, rows // n, feature)).reshape(rows, feature)
    return lax.all_to_all(copies, NAMES, split_axis=0, concat_axis=0, tiled=True)


def split(outputs):
    return outputs[:2], outputs[2:]


def per_device(tokens, slot_params, expert_in, expert_out, grad_out):
    n_expert = lax.axis_size(EXPERT)
    resident = expert_in.shape[0]
    outgoing, p_dispatch, p_combine = route(tokens, slot_params, grad_out, n_expert)
    first, second = sort_rows(exchange(outgoing), n_expert, resident)
    one, two, weights = gather(first, second, expert_in, expert_out)
    kept_one, partial_one = split(expert_call(one, *weights, 0))
    sums_one = reduce(partial_one, up, "sum_first")
    kept_two, partial_two = split(expert_call(two, *weights, resident // 2))
    sums_two = reduce(partial_two, down, "sum_second")
    grad_w_out, grad_w_in = weight_grads((*one, *kept_one), (*two, *kept_two))
    back = exchange(unsort_rows(sums_one, sums_two, n_expert))
    d_logits, local_params, d_slot_in = logits_back(
        tokens, grad_out, back, p_dispatch, p_combine, n_expert
    )
    grad_params = sum_over_all(local_params)
    grad_tokens = tokens_back(p_dispatch, d_slot_in, d_logits, slot_params)
    return (grad_tokens, grad_params, grad_w_in, grad_w_out)


def solution(mesh):
    parts = Mesh(mesh.devices.reshape(2, 4, 2, 2, 4), NAMES)
    image = P(NAMES, None, None)
    weight = P(EXPERT, GROUP, None)
    return jax.shard_map(
        per_device,
        mesh=parts,
        in_specs=(image, P(), weight, weight, image),
        out_specs=(image, P(), weight, weight),
        check_vma=False,
    )
```

```python
import functools
import math

import jax
import jax.numpy as jnp
from jax import lax
from jax.experimental import pallas as pl
from jax.experimental.pallas import tpu as pltpu
from jax.sharding import Mesh, PartitionSpec as P

SLOTS = 2
NAMES = ("yh", "x", "c", "yl", "z")
EXPERT = ("yh", "x", "c")
GROUP = ("yl", "z")
SWAP = [(0, 1), (1, 0)]
BF = jnp.bfloat16
F32 = jnp.float32

inv_root_two = 1.0 / math.sqrt(2.0)
inv_root_tau = 1.0 / math.sqrt(2.0 * math.pi)


def dot(a, b, ca, cb):
    return lax.dot_general(a, b, (((ca,), (cb,)), ((), ())), preferred_element_type=F32)


def params(limit=24):
    return pltpu.CompilerParams(vmem_limit_bytes=limit * 2**20)


def turn(core, z, step):
    return (core * 4 + z, core * 4 + (z + (step if core == 0 else -step)) % 4)


def up(value, name):
    with jax.named_scope(name + "_up"):
        return lax.ppermute(value, ("c", "z"), [turn(c, z, 1) for c in range(2) for z in range(4)])


def down(value, name):
    with jax.named_scope(name + "_down"):
        return lax.ppermute(value, ("c", "z"), [turn(c, z, -1) for c in range(2) for z in range(4)])


def across(value, name):
    with jax.named_scope(name + "_across"):
        return lax.ppermute(value, "yl", SWAP)


def one_hot_rows(rows, n_expert, resident):
    r = lax.broadcasted_iota(jnp.int32, (rows, rows), 0)
    k = lax.broadcasted_iota(jnp.int32, (rows, rows), 1)
    per = n_expert * SLOTS
    e, kind, source, s = r // (2 * per), r // per % 2, r % per // SLOTS, r % SLOTS
    wanted = ((source * 2 + kind) * resident + e) * SLOTS + s
    return (k == wanted).astype(F32).astype(BF)


def route_kernel(n_expert, tokens, slot_params, grad_out, rows, p_dispatch, p_combine):
    t = tokens[0]
    slots, feature = slot_params.shape
    logits = dot(slot_params[...], t, 1, 1)
    wide = jnp.exp(logits - jnp.max(logits, axis=1, keepdims=True))
    pd = wide / jnp.sum(wide, axis=1, keepdims=True)
    p_dispatch[...] = pd
    tall = jnp.exp(logits - jnp.max(logits, axis=0, keepdims=True))
    pc = tall / jnp.sum(tall, axis=0, keepdims=True)
    p_combine[...] = pc
    shape = (n_expert, slots // n_expert, feature)
    slot_in = dot(pd.astype(BF), t, 1, 0).reshape(shape)
    d_slot_out = dot(pc.astype(BF), grad_out[0], 1, 0).reshape(shape)
    both = jnp.concatenate([slot_in, d_slot_out], axis=1).astype(BF)
    rows[...] = both.reshape(rows.shape)


def route(tokens, slot_params, grad_out, n_expert):
    _, length, feature = tokens.shape
    slots = slot_params.shape[0]
    rows = jax.ShapeDtypeStruct((2 * slots, feature), BF)
    probs = jax.ShapeDtypeStruct((slots, length), F32)
    return pl.pallas_call(
        functools.partial(route_kernel, n_expert),
        out_shape=(rows, probs, probs),
        compiler_params=params(60),
        name="route",
    )(tokens, slot_params, grad_out)


def sort_kernel(n_expert, resident, rows, first, second):
    n = rows.shape[0]
    out = dot(one_hot_rows(n, n_expert, resident), rows[...], 1, 0).astype(BF)
    half = out.reshape(2, *first.shape)
    first[...] = half[0]
    second[...] = half[1]


def sort_rows(rows, n_expert, resident):
    n, feature = rows.shape
    half = jax.ShapeDtypeStruct((resident // 2, n // resident, feature), BF)
    return pl.pallas_call(
        functools.partial(sort_kernel, n_expert, resident),
        out_shape=(half, half),
        compiler_params=params(),
        name="sort_rows",
    )(rows)


def after(values, others):
    return lax.optimization_barrier((tuple(values), tuple(others)))[0]


def stage_kernel(w_in, w_out, near_in, near_out, sems):
    copies = [
        pltpu.make_async_copy(w_in, near_in, sems.at[0]),
        pltpu.make_async_copy(w_out, near_out, sems.at[1]),
    ]
    for copy in copies:
        copy.start()
    for copy in copies:
        copy.wait()


def stage(w_in, w_out):
    return pl.pallas_call(
        stage_kernel,
        in_specs=[pl.BlockSpec(memory_space=pltpu.HBM)] * 2,
        out_specs=[pl.BlockSpec(memory_space=pl.ANY)] * 2,
        out_shape=[jax.ShapeDtypeStruct(w.shape, w.dtype) for w in (w_in, w_out)],
        scratch_shapes=[pltpu.SemaphoreType.DMA((2,))],
        compiler_params=params(40),
        name="stage",
    )(w_in, w_out)


def gather(first, second, w_in, w_out):
    low1, high1, y1 = up(first, "first"), down(first, "first"), across(first, "first")
    low2, high2, y2 = up(second, "second"), down(second, "second"), across(second, "second")
    far1, far2 = up(low1, "first_on"), down(high2, "second_on")
    weights = stage(*after((w_in, w_out), (low1, high1)))
    y_low1, y_high1 = up(y1, "first_y"), down(y1, "first_y")
    (sent,) = after((far1,), weights)
    one = (first, low1, far1, high1, y1, y_low1, across(sent, "first_far"), y_high1)
    (y2,) = after((y2,), (far1,))
    y_low2, y_high2 = up(y2, "second_y"), down(y2, "second_y")
    two = (second, low2, far2, high2, y2, y_low2, across(far2, "second_far"), y_high2)
    return one, two, weights


def assemble(refs, into):
    part = refs[0].shape[1] // 2
    for place, ref in enumerate(refs):
        for kind in range(2):
            into[kind, place * part : (place + 1) * part] = ref[0, kind * part : (kind + 1) * part]


def scatter_out(kind, total, refs):
    part = refs[0].shape[1] // 2
    for place, ref in enumerate(refs):
        ref[0, kind * part : (kind + 1) * part] = total[place * part : (place + 1) * part]


def expert_kernel(*refs):
    pieces, (w_in, w_out), (active, d_hidden) = refs[:8], refs[8:10], refs[10:12]
    partial, rows = refs[12:20], refs[20]
    assemble(pieces, rows)
    hidden = dot(w_in[0], rows[0], 1, 1)
    d_active = dot(w_out[0], rows[1], 1, 1)
    bell = 0.5 * (1.0 + lax.erf(hidden * inv_root_two))
    act = (hidden * bell).astype(BF)
    active[0] = act
    slope = bell + hidden * jnp.exp(-0.5 * hidden * hidden) * inv_root_tau
    dh = (d_active * slope).astype(BF)
    d_hidden[0] = dh
    scatter_out(0, dot(act, w_out[0], 0, 0).astype(BF), partial)
    scatter_out(1, dot(dh, w_in[0], 0, 0).astype(BF), partial)


def per_expert(*shape, base=0):
    return pl.BlockSpec((1, *shape), lambda e: (e + base, 0, 0))


def expert_call(pieces, w_in, w_out, base):
    _, hid, feature = w_in.shape
    count, block, _ = pieces[0].shape
    total = 4 * block
    work = count * hid * total * feature
    return pl.pallas_call(
        expert_kernel,
        grid=(count,),
        in_specs=[per_expert(block, feature)] * 8 + [per_expert(hid, feature, base=base)] * 2,
        out_specs=[per_expert(hid, total)] * 2 + [per_expert(block, feature)] * 8,
        out_shape=[jax.ShapeDtypeStruct((count, hid, total), BF)] * 2
        + [jax.ShapeDtypeStruct((count, block, feature), BF)] * 8,
        scratch_shapes=[pltpu.VMEM((2, total, feature), BF)],
        compiler_params=params(24),
        cost_estimate=pl.CostEstimate(flops=8 * work, bytes_accessed=12 * 2**20, transcendentals=0),
        name="expert",
    )(*pieces, w_in, w_out)


def weights_kernel(half, *refs):
    one, two = refs[:10], refs[10:20]
    grad_w_out, grad_w_in, rows = refs[20:]

    def work(pieces, active, d_hidden):
        assemble(pieces, rows)
        grad_w_out[0] = dot(active[0], rows[1], 1, 0).astype(BF)
        grad_w_in[0] = dot(d_hidden[0], rows[0], 1, 0).astype(BF)

    @pl.when(pl.program_id(0) < half)
    def _():
        work(one[:8], *one[8:])

    @pl.when(pl.program_id(0) >= half)
    def _():
        work(two[:8], *two[8:])


def weight_grads(one, two):
    half, hid, total = one[8].shape
    block, feature = one[0].shape[1:]

    def first(*shape):
        return pl.BlockSpec((1, *shape), lambda e: (jnp.minimum(e, half - 1), 0, 0))

    def second(*shape):
        return pl.BlockSpec((1, *shape), lambda e: (jnp.maximum(e - half, 0), 0, 0))

    in_specs = []
    for spec in (first, second):
        in_specs += [spec(block, feature)] * 8 + [spec(hid, total)] * 2
    out = jax.ShapeDtypeStruct((2 * half, hid, feature), BF)
    work = 2 * half * hid * total * feature
    return pl.pallas_call(
        functools.partial(weights_kernel, half),
        grid=(2 * half,),
        in_specs=in_specs,
        out_specs=[per_expert(hid, feature)] * 2,
        out_shape=[out, out],
        scratch_shapes=[pltpu.VMEM((2, total, feature), BF)],
        compiler_params=params(60),
        cost_estimate=pl.CostEstimate(flops=4 * work, bytes_accessed=20 * 2**20, transcendentals=0),
        name="weight_grads",
    )(*one, *two)


def add(*values):
    return sum(v.astype(F32) for v in values).astype(BF)


def reduce(parts, far_way, name, wait=False):
    own, low, far, high, y, y_low, y_far, y_high = parts
    w = across(y_far, name + "_far")
    v_up, v_down = up(y_high, name + "_y"), down(y_low, name + "_y")
    near, last, other_way = (low, high, down) if far_way is up else (high, low, up)
    h = far_way(add(far, w), name + "_on")
    if wait:
        (near,) = after((near,), (h,))
    direct = other_way(near, name)
    chain = far_way(add(last, h), name)
    if not wait:
        y, v_up, v_down = after((y, v_up, v_down), (direct,))
    return own, direct, chain, across(add(y, v_up, v_down), name)


def unsort_kernel(n_expert, n_first, *refs):
    out = refs[-1]
    half, block, feature = refs[0].shape
    n = 2 * half * block
    first = sum(ref[...].astype(F32) for ref in refs[:n_first])
    second = sum(ref[...].astype(F32) for ref in refs[n_first:-1])
    total = jnp.concatenate([first, second], axis=0).reshape(n, feature).astype(BF)
    out[...] = dot(one_hot_rows(n, n_expert, 2 * half), total, 0, 0).astype(BF)


def unsort_rows(first, second, n_expert):
    half, block, feature = first[0].shape
    return pl.pallas_call(
        functools.partial(unsort_kernel, n_expert, len(first)),
        out_shape=jax.ShapeDtypeStruct((2 * half * block, feature), BF),
        compiler_params=params(),
        name="unsort_rows",
    )(*first, *second)


def exchange(rows):
    return lax.all_to_all(rows, EXPERT, split_axis=0, concat_axis=0, tiled=True)


def logits_kernel(n_expert, tokens, grad_out, back, p_dispatch, p_combine, d_logits, local, d_slot):
    t = tokens[0]
    n, feature = back.shape
    wide = back[...].astype(F32).reshape(n_expert, n // n_expert, feature)
    split = n // n_expert // 2
    slot_out = wide[:, :split].reshape(n // 2, feature).astype(BF)
    d_slot_in = wide[:, split:].reshape(n // 2, feature).astype(BF)
    d_slot[...] = d_slot_in
    d_combine = dot(slot_out, grad_out[0], 1, 1)
    d_dispatch = dot(d_slot_in, t, 1, 1)
    pd, pc = p_dispatch[...], p_combine[...]
    grad = pd * (d_dispatch - jnp.sum(pd * d_dispatch, axis=1, keepdims=True)) + pc * (
        d_combine - jnp.sum(pc * d_combine, axis=0, keepdims=True)
    )
    dl = grad.astype(BF)
    d_logits[...] = dl
    local[...] = dot(dl, t, 1, 0)


def logits_back(tokens, grad_out, back, p_dispatch, p_combine, n_expert):
    slots = p_dispatch.shape[0]
    feature = back.shape[1]
    return pl.pallas_call(
        functools.partial(logits_kernel, n_expert),
        out_shape=(
            jax.ShapeDtypeStruct(p_dispatch.shape, BF),
            jax.ShapeDtypeStruct((slots, feature), F32),
            jax.ShapeDtypeStruct((slots, feature), BF),
        ),
        compiler_params=params(),
        name="logits_back",
    )(tokens, grad_out, back, p_dispatch, p_combine)


def tokens_kernel(p_dispatch, d_slot_in, d_logits, slot_params, grad_tokens):
    first = dot(p_dispatch[...].astype(BF), d_slot_in[...], 0, 0)
    second = dot(d_logits[...], slot_params[...], 0, 0)
    grad_tokens[0] = (first + second).astype(BF)


def tokens_back(p_dispatch, d_slot_in, d_logits, slot_params):
    slots, length = p_dispatch.shape
    feature = slot_params.shape[1]
    return pl.pallas_call(
        tokens_kernel,
        out_shape=jax.ShapeDtypeStruct((1, length, feature), BF),
        compiler_params=params(),
        name="tokens_back",
    )(p_dispatch, d_slot_in, d_logits, slot_params)


def sum_over_all(value):
    n = lax.axis_size(NAMES)
    rows, feature = value.shape
    terms = lax.all_to_all(value, NAMES, split_axis=0, concat_axis=0, tiled=True)
    mine = jnp.sum(terms.reshape(n, rows // n, feature), axis=0)
    copies = jnp.broadcast_to(mine[None], (n, rows // n, feature)).reshape(rows, feature)
    return lax.all_to_all(copies, NAMES, split_axis=0, concat_axis=0, tiled=True)


def split(outputs):
    return outputs[:2], outputs[2:]


def per_device(tokens, slot_params, expert_in, expert_out, grad_out):
    n_expert = lax.axis_size(EXPERT)
    resident = expert_in.shape[0]
    outgoing, p_dispatch, p_combine = route(tokens, slot_params, grad_out, n_expert)
    first, second = sort_rows(exchange(outgoing), n_expert, resident)
    one, two, weights = gather(first, second, expert_in, expert_out)
    kept_one, partial_one = split(expert_call(one, *weights, 0))
    sums_one = reduce(partial_one, up, "sum_first")
    kept_two, partial_two = split(expert_call(two, *weights, resident // 2))
    sums_two = reduce(partial_two, down, "sum_second", True)
    grad_w_out, grad_w_in = weight_grads((*one, *kept_one), (*two, *kept_two))
    back = exchange(unsort_rows(sums_one, sums_two, n_expert))
    d_logits, local_params, d_slot_in = logits_back(
        tokens, grad_out, back, p_dispatch, p_combine, n_expert
    )
    grad_params = sum_over_all(local_params)
    grad_tokens = tokens_back(p_dispatch, d_slot_in, d_logits, slot_params)
    return (grad_tokens, grad_params, grad_w_in, grad_w_out)


def solution(mesh):
    parts = Mesh(mesh.devices.reshape(2, 4, 2, 2, 4), NAMES)
    image = P(NAMES, None, None)
    weight = P(EXPERT, GROUP, None)
    return jax.shard_map(
        per_device,
        mesh=parts,
        in_specs=(image, P(), weight, weight, image),
        out_specs=(image, P(), weight, weight),
        check_vma=False,
    )
```

```python
import functools
import math

import jax
import jax.numpy as jnp
from jax import lax
from jax.experimental import pallas as pl
from jax.experimental.pallas import tpu as pltpu
from jax.sharding import Mesh, PartitionSpec as P

SLOTS = 2
NAMES = ("yh", "x", "c", "yl", "z")
EXPERT = ("yh", "x", "c")
GROUP = ("yl", "z")
SWAP = [(0, 1), (1, 0)]
BF = jnp.bfloat16
F32 = jnp.float32

inv_root_two = 1.0 / math.sqrt(2.0)
inv_root_tau = 1.0 / math.sqrt(2.0 * math.pi)


def dot(a, b, ca, cb):
    return lax.dot_general(a, b, (((ca,), (cb,)), ((), ())), preferred_element_type=F32)


def params(limit=24):
    return pltpu.CompilerParams(vmem_limit_bytes=limit * 2**20)


def turn(core, z, step):
    return (core * 4 + z, core * 4 + (z + (step if core == 0 else -step)) % 4)


def up(value, name):
    with jax.named_scope(name + "_up"):
        return lax.ppermute(value, ("c", "z"), [turn(c, z, 1) for c in range(2) for z in range(4)])


def down(value, name):
    with jax.named_scope(name + "_down"):
        return lax.ppermute(value, ("c", "z"), [turn(c, z, -1) for c in range(2) for z in range(4)])


def across(value, name):
    with jax.named_scope(name + "_across"):
        return lax.ppermute(value, "yl", SWAP)


def one_hot_rows(rows, n_expert, resident):
    r = lax.broadcasted_iota(jnp.int32, (rows, rows), 0)
    k = lax.broadcasted_iota(jnp.int32, (rows, rows), 1)
    per = n_expert * SLOTS
    e, kind, source, s = r // (2 * per), r // per % 2, r % per // SLOTS, r % SLOTS
    wanted = ((source * 2 + kind) * resident + e) * SLOTS + s
    return (k == wanted).astype(F32).astype(BF)


def route_kernel(n_expert, tokens, slot_params, grad_out, rows, p_dispatch, p_combine):
    t = tokens[0]
    slots, feature = slot_params.shape
    logits = dot(slot_params[...], t, 1, 1)
    wide = jnp.exp(logits - jnp.max(logits, axis=1, keepdims=True))
    pd = wide / jnp.sum(wide, axis=1, keepdims=True)
    p_dispatch[...] = pd
    tall = jnp.exp(logits - jnp.max(logits, axis=0, keepdims=True))
    pc = tall / jnp.sum(tall, axis=0, keepdims=True)
    p_combine[...] = pc
    shape = (n_expert, slots // n_expert, feature)
    slot_in = dot(pd.astype(BF), t, 1, 0).reshape(shape)
    d_slot_out = dot(pc.astype(BF), grad_out[0], 1, 0).reshape(shape)
    both = jnp.concatenate([slot_in, d_slot_out], axis=1).astype(BF)
    rows[...] = both.reshape(rows.shape)


def route(tokens, slot_params, grad_out, n_expert):
    _, length, feature = tokens.shape
    slots = slot_params.shape[0]
    rows = jax.ShapeDtypeStruct((2 * slots, feature), BF)
    probs = jax.ShapeDtypeStruct((slots, length), F32)
    return pl.pallas_call(
        functools.partial(route_kernel, n_expert),
        out_shape=(rows, probs, probs),
        compiler_params=params(60),
        name="route",
    )(tokens, slot_params, grad_out)


def sort_kernel(n_expert, resident, rows, first, second):
    n = rows.shape[0]
    out = dot(one_hot_rows(n, n_expert, resident), rows[...], 1, 0).astype(BF)
    half = out.reshape(2, *first.shape)
    first[...] = half[0]
    second[...] = half[1]


def sort_rows(rows, n_expert, resident):
    n, feature = rows.shape
    half = jax.ShapeDtypeStruct((resident // 2, n // resident, feature), BF)
    return pl.pallas_call(
        functools.partial(sort_kernel, n_expert, resident),
        out_shape=(half, half),
        compiler_params=params(),
        name="sort_rows",
    )(rows)


def after(values, others):
    return lax.optimization_barrier((tuple(values), tuple(others)))[0]


def stage_kernel(w_in, w_out, near_in, near_out, sems):
    copies = [
        pltpu.make_async_copy(w_in, near_in, sems.at[0]),
        pltpu.make_async_copy(w_out, near_out, sems.at[1]),
    ]
    for copy in copies:
        copy.start()
    for copy in copies:
        copy.wait()


def stage(w_in, w_out):
    return pl.pallas_call(
        stage_kernel,
        in_specs=[pl.BlockSpec(memory_space=pltpu.HBM)] * 2,
        out_specs=[pl.BlockSpec(memory_space=pl.ANY)] * 2,
        out_shape=[jax.ShapeDtypeStruct(w.shape, w.dtype) for w in (w_in, w_out)],
        scratch_shapes=[pltpu.SemaphoreType.DMA((2,))],
        compiler_params=params(40),
        name="stage",
    )(w_in, w_out)


def gather(first, second, w_in, w_out):
    low1, high1, y1 = up(first, "first"), down(first, "first"), across(first, "first")
    low2, high2, y2 = up(second, "second"), down(second, "second"), across(second, "second")
    far1, far2 = up(low1, "first_on"), down(high2, "second_on")
    (y1,) = after((y1,), (high1,))
    y_low1, y_high1 = up(y1, "first_y"), down(y1, "first_y")
    weights = stage(*after((w_in, w_out), (y_low1,)))
    one = (first, low1, far1, high1, y1, y_low1, across(far1, "first_far"), y_high1)
    (y2,) = after((y2,), (far1,))
    y_low2, y_high2 = up(y2, "second_y"), down(y2, "second_y")
    (far2,) = after((far2,), weights)
    two = (second, low2, far2, high2, y2, y_low2, across(far2, "second_far"), y_high2)
    return one, two, weights


def assemble(refs, into):
    part = refs[0].shape[1] // 2
    for place, ref in enumerate(refs):
        for kind in range(2):
            into[kind, place * part : (place + 1) * part] = ref[0, kind * part : (kind + 1) * part]


def scatter_out(kind, total, refs):
    part = refs[0].shape[1] // 2
    for place, ref in enumerate(refs):
        ref[0, kind * part : (kind + 1) * part] = total[place * part : (place + 1) * part]


def expert_kernel(*refs):
    pieces, (w_in, w_out), (active, d_hidden) = refs[:8], refs[8:10], refs[10:12]
    partial, rows = refs[12:20], refs[20]
    assemble(pieces, rows)
    hidden = dot(w_in[0], rows[0], 1, 1)
    d_active = dot(w_out[0], rows[1], 1, 1)
    bell = 0.5 * (1.0 + lax.erf(hidden * inv_root_two))
    act = (hidden * bell).astype(BF)
    active[0] = act
    slope = bell + hidden * jnp.exp(-0.5 * hidden * hidden) * inv_root_tau
    dh = (d_active * slope).astype(BF)
    d_hidden[0] = dh
    scatter_out(0, dot(act, w_out[0], 0, 0).astype(BF), partial)
    scatter_out(1, dot(dh, w_in[0], 0, 0).astype(BF), partial)


def per_expert(*shape, base=0):
    return pl.BlockSpec((1, *shape), lambda e: (e + base, 0, 0))


def expert_call(pieces, w_in, w_out, base):
    _, hid, feature = w_in.shape
    count, block, _ = pieces[0].shape
    total = 4 * block
    work = count * hid * total * feature
    return pl.pallas_call(
        expert_kernel,
        grid=(count,),
        in_specs=[per_expert(block, feature)] * 8 + [per_expert(hid, feature, base=base)] * 2,
        out_specs=[per_expert(hid, total)] * 2 + [per_expert(block, feature)] * 8,
        out_shape=[jax.ShapeDtypeStruct((count, hid, total), BF)] * 2
        + [jax.ShapeDtypeStruct((count, block, feature), BF)] * 8,
        scratch_shapes=[pltpu.VMEM((2, total, feature), BF)],
        compiler_params=params(24),
        cost_estimate=pl.CostEstimate(flops=8 * work, bytes_accessed=12 * 2**20, transcendentals=0),
        name="expert",
    )(*pieces, w_in, w_out)


def weights_kernel(half, *refs):
    one, two = refs[:10], refs[10:20]
    grad_w_out, grad_w_in, rows = refs[20:]

    def work(pieces, active, d_hidden):
        assemble(pieces, rows)
        grad_w_out[0] = dot(active[0], rows[1], 1, 0).astype(BF)
        grad_w_in[0] = dot(d_hidden[0], rows[0], 1, 0).astype(BF)

    @pl.when(pl.program_id(0) < half)
    def _():
        work(one[:8], *one[8:])

    @pl.when(pl.program_id(0) >= half)
    def _():
        work(two[:8], *two[8:])


def weight_grads(one, two):
    half, hid, total = one[8].shape
    block, feature = one[0].shape[1:]

    def first(*shape):
        return pl.BlockSpec((1, *shape), lambda e: (jnp.minimum(e, half - 1), 0, 0))

    def second(*shape):
        return pl.BlockSpec((1, *shape), lambda e: (jnp.maximum(e - half, 0), 0, 0))

    in_specs = []
    for spec in (first, second):
        in_specs += [spec(block, feature)] * 8 + [spec(hid, total)] * 2
    out = jax.ShapeDtypeStruct((2 * half, hid, feature), BF)
    work = 2 * half * hid * total * feature
    return pl.pallas_call(
        functools.partial(weights_kernel, half),
        grid=(2 * half,),
        in_specs=in_specs,
        out_specs=[per_expert(hid, feature)] * 2,
        out_shape=[out, out],
        scratch_shapes=[pltpu.VMEM((2, total, feature), BF)],
        compiler_params=params(60),
        cost_estimate=pl.CostEstimate(flops=4 * work, bytes_accessed=20 * 2**20, transcendentals=0),
        name="weight_grads",
    )(*one, *two)


def add(*values):
    return sum(v.astype(F32) for v in values).astype(BF)


def reduce(parts, far_way, name, wait=False):
    own, low, far, high, y, y_low, y_far, y_high = parts
    w = across(y_far, name + "_far")
    v_up, v_down = up(y_high, name + "_y"), down(y_low, name + "_y")
    near, last, other_way = (low, high, down) if far_way is up else (high, low, up)
    h = far_way(add(far, w), name + "_on")
    if wait:
        (near,) = after((near,), (h,))
    direct = other_way(near, name)
    chain = far_way(add(last, h), name)
    if not wait:
        y, v_up, v_down = after((y, v_up, v_down), (direct,))
    return own, direct, chain, across(add(y, v_up, v_down), name)


def unsort_kernel(n_expert, n_first, *refs):
    out = refs[-1]
    half, block, feature = refs[0].shape
    n = 2 * half * block
    first = sum(ref[...].astype(F32) for ref in refs[:n_first])
    second = sum(ref[...].astype(F32) for ref in refs[n_first:-1])
    total = jnp.concatenate([first, second], axis=0).reshape(n, feature).astype(BF)
    out[...] = dot(one_hot_rows(n, n_expert, 2 * half), total, 0, 0).astype(BF)


def unsort_rows(first, second, n_expert):
    half, block, feature = first[0].shape
    return pl.pallas_call(
        functools.partial(unsort_kernel, n_expert, len(first)),
        out_shape=jax.ShapeDtypeStruct((2 * half * block, feature), BF),
        compiler_params=params(),
        name="unsort_rows",
    )(*first, *second)


def exchange(rows):
    return lax.all_to_all(rows, EXPERT, split_axis=0, concat_axis=0, tiled=True)


def logits_kernel(n_expert, tokens, grad_out, back, p_dispatch, p_combine, d_logits, local, d_slot):
    t = tokens[0]
    n, feature = back.shape
    wide = back[...].astype(F32).reshape(n_expert, n // n_expert, feature)
    split = n // n_expert // 2
    slot_out = wide[:, :split].reshape(n // 2, feature).astype(BF)
    d_slot_in = wide[:, split:].reshape(n // 2, feature).astype(BF)
    d_slot[...] = d_slot_in
    d_combine = dot(slot_out, grad_out[0], 1, 1)
    d_dispatch = dot(d_slot_in, t, 1, 1)
    pd, pc = p_dispatch[...], p_combine[...]
    grad = pd * (d_dispatch - jnp.sum(pd * d_dispatch, axis=1, keepdims=True)) + pc * (
        d_combine - jnp.sum(pc * d_combine, axis=0, keepdims=True)
    )
    dl = grad.astype(BF)
    d_logits[...] = dl
    local[...] = dot(dl, t, 1, 0)


def logits_back(tokens, grad_out, back, p_dispatch, p_combine, n_expert):
    slots = p_dispatch.shape[0]
    feature = back.shape[1]
    return pl.pallas_call(
        functools.partial(logits_kernel, n_expert),
        out_shape=(
            jax.ShapeDtypeStruct(p_dispatch.shape, BF),
            jax.ShapeDtypeStruct((slots, feature), F32),
            jax.ShapeDtypeStruct((slots, feature), BF),
        ),
        compiler_params=params(),
        name="logits_back",
    )(tokens, grad_out, back, p_dispatch, p_combine)


def tokens_kernel(p_dispatch, d_slot_in, d_logits, slot_params, grad_tokens):
    first = dot(p_dispatch[...].astype(BF), d_slot_in[...], 0, 0)
    second = dot(d_logits[...], slot_params[...], 0, 0)
    grad_tokens[0] = (first + second).astype(BF)


def tokens_back(p_dispatch, d_slot_in, d_logits, slot_params):
    slots, length = p_dispatch.shape
    feature = slot_params.shape[1]
    return pl.pallas_call(
        tokens_kernel,
        out_shape=jax.ShapeDtypeStruct((1, length, feature), BF),
        compiler_params=params(),
        name="tokens_back",
    )(p_dispatch, d_slot_in, d_logits, slot_params)


def sum_over_all(value):
    n = lax.axis_size(NAMES)
    rows, feature = value.shape
    terms = lax.all_to_all(value, NAMES, split_axis=0, concat_axis=0, tiled=True)
    mine = jnp.sum(terms.reshape(n, rows // n, feature), axis=0)
    copies = jnp.broadcast_to(mine[None], (n, rows // n, feature)).reshape(rows, feature)
    return lax.all_to_all(copies, NAMES, split_axis=0, concat_axis=0, tiled=True)


def split(outputs):
    return outputs[:2], outputs[2:]


def per_device(tokens, slot_params, expert_in, expert_out, grad_out):
    n_expert = lax.axis_size(EXPERT)
    resident = expert_in.shape[0]
    outgoing, p_dispatch, p_combine = route(tokens, slot_params, grad_out, n_expert)
    first, second = sort_rows(exchange(outgoing), n_expert, resident)
    one, two, weights = gather(first, second, expert_in, expert_out)
    kept_one, partial_one = split(expert_call(one, *weights, 0))
    sums_one = reduce(partial_one, up, "sum_first")
    kept_two, partial_two = split(expert_call(two, *weights, resident // 2))
    sums_two = reduce(partial_two, down, "sum_second", True)
    grad_w_out, grad_w_in = weight_grads((*one, *kept_one), (*two, *kept_two))
    back = exchange(unsort_rows(sums_one, sums_two, n_expert))
    d_logits, local_params, d_slot_in = logits_back(
        tokens, grad_out, back, p_dispatch, p_combine, n_expert
    )
    grad_params = sum_over_all(local_params)
    grad_tokens = tokens_back(p_dispatch, d_slot_in, d_logits, slot_params)
    return (grad_tokens, grad_params, grad_w_in, grad_w_out)


def solution(mesh):
    parts = Mesh(mesh.devices.reshape(2, 4, 2, 2, 4), NAMES)
    image = P(NAMES, None, None)
    weight = P(EXPERT, GROUP, None)
    return jax.shard_map(
        per_device,
        mesh=parts,
        in_specs=(image, P(), weight, weight, image),
        out_specs=(image, P(), weight, weight),
        check_vma=False,
    )
```

```python
import functools
import math

import jax
import jax.numpy as jnp
from jax import lax
from jax.experimental import pallas as pl
from jax.experimental.pallas import tpu as pltpu
from jax.sharding import Mesh, PartitionSpec as P

SLOTS = 2
NAMES = ("yh", "x", "c", "yl", "z")
EXPERT = ("yh", "x", "c")
GROUP = ("yl", "z")
SWAP = [(0, 1), (1, 0)]
BF = jnp.bfloat16
F32 = jnp.float32

inv_root_two = 1.0 / math.sqrt(2.0)
inv_root_tau = 1.0 / math.sqrt(2.0 * math.pi)


def dot(a, b, ca, cb):
    return lax.dot_general(a, b, (((ca,), (cb,)), ((), ())), preferred_element_type=F32)


def params(limit=24):
    return pltpu.CompilerParams(vmem_limit_bytes=limit * 2**20)


def turn(core, z, step):
    return (core * 4 + z, core * 4 + (z + (step if core == 0 else -step)) % 4)


def up(value, name):
    with jax.named_scope(name + "_up"):
        return lax.ppermute(value, ("c", "z"), [turn(c, z, 1) for c in range(2) for z in range(4)])


def down(value, name):
    with jax.named_scope(name + "_down"):
        return lax.ppermute(value, ("c", "z"), [turn(c, z, -1) for c in range(2) for z in range(4)])


def across(value, name):
    with jax.named_scope(name + "_across"):
        return lax.ppermute(value, "yl", SWAP)


def one_hot_rows(rows, n_expert, resident):
    r = lax.broadcasted_iota(jnp.int32, (rows, rows), 0)
    k = lax.broadcasted_iota(jnp.int32, (rows, rows), 1)
    per = n_expert * SLOTS
    e, kind, source, s = r // (2 * per), r // per % 2, r % per // SLOTS, r % SLOTS
    wanted = ((source * 2 + kind) * resident + e) * SLOTS + s
    return (k == wanted).astype(F32).astype(BF)


def route_kernel(n_expert, tokens, slot_params, grad_out, rows, p_dispatch, p_combine):
    t = tokens[0]
    slots, feature = slot_params.shape
    logits = dot(slot_params[...], t, 1, 1)
    wide = jnp.exp(logits - jnp.max(logits, axis=1, keepdims=True))
    pd = wide / jnp.sum(wide, axis=1, keepdims=True)
    p_dispatch[...] = pd
    tall = jnp.exp(logits - jnp.max(logits, axis=0, keepdims=True))
    pc = tall / jnp.sum(tall, axis=0, keepdims=True)
    p_combine[...] = pc
    shape = (n_expert, slots // n_expert, feature)
    slot_in = dot(pd.astype(BF), t, 1, 0).reshape(shape)
    d_slot_out = dot(pc.astype(BF), grad_out[0], 1, 0).reshape(shape)
    both = jnp.concatenate([slot_in, d_slot_out], axis=1).astype(BF)
    rows[...] = both.reshape(rows.shape)


def route(tokens, slot_params, grad_out, n_expert):
    _, length, feature = tokens.shape
    slots = slot_params.shape[0]
    rows = jax.ShapeDtypeStruct((2 * slots, feature), BF)
    probs = jax.ShapeDtypeStruct((slots, length), F32)
    return pl.pallas_call(
        functools.partial(route_kernel, n_expert),
        out_shape=(rows, probs, probs),
        compiler_params=params(60),
        name="route",
    )(tokens, slot_params, grad_out)


def sort_kernel(n_expert, resident, rows, first, second):
    n = rows.shape[0]
    out = dot(one_hot_rows(n, n_expert, resident), rows[...], 1, 0).astype(BF)
    half = out.reshape(2, *first.shape)
    first[...] = half[0]
    second[...] = half[1]


def sort_rows(rows, n_expert, resident):
    n, feature = rows.shape
    half = jax.ShapeDtypeStruct((resident // 2, n // resident, feature), BF)
    return pl.pallas_call(
        functools.partial(sort_kernel, n_expert, resident),
        out_shape=(half, half),
        compiler_params=params(),
        name="sort_rows",
    )(rows)


def after(values, others):
    return lax.optimization_barrier((tuple(values), tuple(others)))[0]


def stage_kernel(w_in, w_out, near_in, near_out, sems):
    copies = [
        pltpu.make_async_copy(w_in, near_in, sems.at[0]),
        pltpu.make_async_copy(w_out, near_out, sems.at[1]),
    ]
    for copy in copies:
        copy.start()
    for copy in copies:
        copy.wait()


def stage(w_in, w_out):
    return pl.pallas_call(
        stage_kernel,
        in_specs=[pl.BlockSpec(memory_space=pltpu.HBM)] * 2,
        out_specs=[pl.BlockSpec(memory_space=pl.ANY)] * 2,
        out_shape=[jax.ShapeDtypeStruct(w.shape, w.dtype) for w in (w_in, w_out)],
        scratch_shapes=[pltpu.SemaphoreType.DMA((2,))],
        compiler_params=params(40),
        name="stage",
    )(w_in, w_out)


def gather(first, second, w_in, w_out):
    low1, high1, y1 = up(first, "first"), down(first, "first"), across(first, "first")
    low2, high2, y2 = up(second, "second"), down(second, "second"), across(second, "second")
    far1, far2 = up(low1, "first_on"), down(high2, "second_on")
    (y1,) = after((y1,), (high1,))
    y_low1, y_high1 = up(y1, "first_y"), down(y1, "first_y")
    weights = stage(*after((w_in, w_out), (y_low1,)))
    one = (first, low1, far1, high1, y1, y_low1, across(far1, "first_far"), y_high1)
    (y2,) = after((y2,), (far1,))
    y_low2, y_high2 = up(y2, "second_y"), down(y2, "second_y")
    (far2,) = after((far2,), weights)
    two = (second, low2, far2, high2, y2, y_low2, across(far2, "second_far"), y_high2)
    return one, two, weights


def assemble(refs, into):
    part = refs[0].shape[1] // 2
    for place, ref in enumerate(refs):
        for kind in range(2):
            into[kind, place * part : (place + 1) * part] = ref[0, kind * part : (kind + 1) * part]


def scatter_out(kind, total, refs):
    part = refs[0].shape[1] // 2
    for place, ref in enumerate(refs):
        ref[0, kind * part : (kind + 1) * part] = total[place * part : (place + 1) * part]


def expert_kernel(*refs):
    pieces, (w_in, w_out), (active, d_hidden) = refs[:8], refs[8:10], refs[10:12]
    partial, rows = refs[12:20], refs[20]
    assemble(pieces, rows)
    hidden = dot(w_in[0], rows[0], 1, 1)
    d_active = dot(w_out[0], rows[1], 1, 1)
    bell = 0.5 * (1.0 + lax.erf(hidden * inv_root_two))
    act = (hidden * bell).astype(BF)
    active[0] = act
    slope = bell + hidden * jnp.exp(-0.5 * hidden * hidden) * inv_root_tau
    dh = (d_active * slope).astype(BF)
    d_hidden[0] = dh
    scatter_out(0, dot(act, w_out[0], 0, 0).astype(BF), partial)
    scatter_out(1, dot(dh, w_in[0], 0, 0).astype(BF), partial)


def per_expert(*shape, base=0):
    return pl.BlockSpec((1, *shape), lambda e: (e + base, 0, 0))


def expert_call(pieces, w_in, w_out, base):
    _, hid, feature = w_in.shape
    count, block, _ = pieces[0].shape
    total = 4 * block
    work = count * hid * total * feature
    return pl.pallas_call(
        expert_kernel,
        grid=(count,),
        in_specs=[per_expert(block, feature)] * 8 + [per_expert(hid, feature, base=base)] * 2,
        out_specs=[per_expert(hid, total)] * 2 + [per_expert(block, feature)] * 8,
        out_shape=[jax.ShapeDtypeStruct((count, hid, total), BF)] * 2
        + [jax.ShapeDtypeStruct((count, block, feature), BF)] * 8,
        scratch_shapes=[pltpu.VMEM((2, total, feature), BF)],
        compiler_params=params(24),
        cost_estimate=pl.CostEstimate(flops=8 * work, bytes_accessed=12 * 2**20, transcendentals=0),
        name="expert",
    )(*pieces, w_in, w_out)


def weights_kernel(half, *refs):
    one, two = refs[:10], refs[10:20]
    grad_w_out, grad_w_in, rows = refs[20:]

    def work(pieces, active, d_hidden):
        assemble(pieces, rows)
        grad_w_out[0] = dot(active[0], rows[1], 1, 0).astype(BF)
        grad_w_in[0] = dot(d_hidden[0], rows[0], 1, 0).astype(BF)

    @pl.when(pl.program_id(0) < half)
    def _():
        work(one[:8], *one[8:])

    @pl.when(pl.program_id(0) >= half)
    def _():
        work(two[:8], *two[8:])


def weight_grads(one, two):
    half, hid, total = one[8].shape
    block, feature = one[0].shape[1:]

    def first(*shape):
        return pl.BlockSpec((1, *shape), lambda e: (jnp.minimum(e, half - 1), 0, 0))

    def second(*shape):
        return pl.BlockSpec((1, *shape), lambda e: (jnp.maximum(e - half, 0), 0, 0))

    in_specs = []
    for spec in (first, second):
        in_specs += [spec(block, feature)] * 8 + [spec(hid, total)] * 2
    out = jax.ShapeDtypeStruct((2 * half, hid, feature), BF)
    work = 2 * half * hid * total * feature
    return pl.pallas_call(
        functools.partial(weights_kernel, half),
        grid=(2 * half,),
        in_specs=in_specs,
        out_specs=[per_expert(hid, feature)] * 2,
        out_shape=[out, out],
        scratch_shapes=[pltpu.VMEM((2, total, feature), BF)],
        compiler_params=params(60),
        cost_estimate=pl.CostEstimate(flops=4 * work, bytes_accessed=20 * 2**20, transcendentals=0),
        name="weight_grads",
    )(*one, *two)


def add(*values):
    return sum(v.astype(F32) for v in values).astype(BF)


def reduce(parts, far_way, name, wait=False):
    own, low, far, high, y, y_low, y_far, y_high = parts
    w = across(y_far, name + "_far")
    v_up, v_down = up(y_high, name + "_y"), down(y_low, name + "_y")
    near, last, other_way = (low, high, down) if far_way is up else (high, low, up)
    h = far_way(add(far, w), name + "_on")
    if wait:
        (near,) = after((near,), (h,))
    direct = other_way(near, name)
    chain = far_way(add(last, h), name)
    if not wait:
        y, v_up, v_down = after((y, v_up, v_down), (direct,))
    return own, direct, chain, across(add(y, v_up, v_down), name)


def unsort_kernel(n_expert, n_first, *refs):
    out = refs[-1]
    half, block, feature = refs[0].shape
    n = 2 * half * block
    first = sum(ref[...].astype(F32) for ref in refs[:n_first])
    second = sum(ref[...].astype(F32) for ref in refs[n_first:-1])
    total = jnp.concatenate([first, second], axis=0).reshape(n, feature).astype(BF)
    out[...] = dot(one_hot_rows(n, n_expert, 2 * half), total, 0, 0).astype(BF)


def unsort_rows(first, second, n_expert):
    half, block, feature = first[0].shape
    return pl.pallas_call(
        functools.partial(unsort_kernel, n_expert, len(first)),
        out_shape=jax.ShapeDtypeStruct((2 * half * block, feature), BF),
        compiler_params=params(),
        name="unsort_rows",
    )(*first, *second)


def exchange(rows):
    return lax.all_to_all(rows, EXPERT, split_axis=0, concat_axis=0, tiled=True)


def logits_kernel(n_expert, tokens, grad_out, back, p_dispatch, p_combine, d_logits, local, d_slot):
    t = tokens[0]
    n, feature = back.shape
    wide = back[...].astype(F32).reshape(n_expert, n // n_expert, feature)
    split = n // n_expert // 2
    slot_out = wide[:, :split].reshape(n // 2, feature).astype(BF)
    d_slot_in = wide[:, split:].reshape(n // 2, feature).astype(BF)
    d_slot[...] = d_slot_in
    d_combine = dot(slot_out, grad_out[0], 1, 1)
    d_dispatch = dot(d_slot_in, t, 1, 1)
    pd, pc = p_dispatch[...], p_combine[...]
    grad = pd * (d_dispatch - jnp.sum(pd * d_dispatch, axis=1, keepdims=True)) + pc * (
        d_combine - jnp.sum(pc * d_combine, axis=0, keepdims=True)
    )
    dl = grad.astype(BF)
    d_logits[...] = dl
    local[...] = dot(dl, t, 1, 0).reshape(local.shape)


def logits_back(tokens, grad_out, back, p_dispatch, p_combine, n_expert):
    slots = p_dispatch.shape[0]
    feature = back.shape[1]
    return pl.pallas_call(
        functools.partial(logits_kernel, n_expert),
        out_shape=(
            jax.ShapeDtypeStruct(p_dispatch.shape, BF),
            jax.ShapeDtypeStruct((slots, 1, feature), F32),
            jax.ShapeDtypeStruct((slots, feature), BF),
        ),
        compiler_params=params(),
        name="logits_back",
    )(tokens, grad_out, back, p_dispatch, p_combine)


def tokens_kernel(p_dispatch, d_slot_in, d_logits, slot_params, grad_tokens):
    first = dot(p_dispatch[...].astype(BF), d_slot_in[...], 0, 0)
    second = dot(d_logits[...], slot_params[...], 0, 0)
    grad_tokens[0] = (first + second).astype(BF)


def tokens_back(p_dispatch, d_slot_in, d_logits, slot_params):
    slots, length = p_dispatch.shape
    feature = slot_params.shape[1]
    return pl.pallas_call(
        tokens_kernel,
        out_shape=jax.ShapeDtypeStruct((1, length, feature), BF),
        compiler_params=params(),
        name="tokens_back",
    )(p_dispatch, d_slot_in, d_logits, slot_params)


def sum_kernel(terms, copies):
    total = jnp.sum(terms[...], axis=0, keepdims=True)
    copies[...] = jnp.broadcast_to(total, copies.shape)


def sum_over_all(value):
    slots, _, feature = value.shape
    terms = lax.all_to_all(value, NAMES, split_axis=0, concat_axis=0, tiled=True)
    copies = pl.pallas_call(
        sum_kernel,
        out_shape=jax.ShapeDtypeStruct(value.shape, F32),
        compiler_params=params(),
        name="sum_terms",
    )(terms)
    total = lax.all_to_all(copies, NAMES, split_axis=0, concat_axis=0, tiled=True)
    return total.reshape(slots, feature)


def split(outputs):
    return outputs[:2], outputs[2:]


def per_device(tokens, slot_params, expert_in, expert_out, grad_out):
    n_expert = lax.axis_size(EXPERT)
    resident = expert_in.shape[0]
    outgoing, p_dispatch, p_combine = route(tokens, slot_params, grad_out, n_expert)
    first, second = sort_rows(exchange(outgoing), n_expert, resident)
    one, two, weights = gather(first, second, expert_in, expert_out)
    kept_one, partial_one = split(expert_call(one, *weights, 0))
    sums_one = reduce(partial_one, up, "sum_first")
    kept_two, partial_two = split(expert_call(two, *weights, resident // 2))
    sums_two = reduce(partial_two, down, "sum_second", True)
    grad_w_out, grad_w_in = weight_grads((*one, *kept_one), (*two, *kept_two))
    back = exchange(unsort_rows(sums_one, sums_two, n_expert))
    d_logits, local_params, d_slot_in = logits_back(
        tokens, grad_out, back, p_dispatch, p_combine, n_expert
    )
    grad_params = sum_over_all(local_params)
    grad_tokens = tokens_back(p_dispatch, d_slot_in, d_logits, slot_params)
    return (grad_tokens, grad_params, grad_w_in, grad_w_out)


def solution(mesh):
    parts = Mesh(mesh.devices.reshape(2, 4, 2, 2, 4), NAMES)
    image = P(NAMES, None, None)
    weight = P(EXPERT, GROUP, None)
    return jax.shard_map(
        per_device,
        mesh=parts,
        in_specs=(image, P(), weight, weight, image),
        out_specs=(image, P(), weight, weight),
        check_vma=False,
    )
```

```python
import functools
import math

import jax
import jax.numpy as jnp
from jax import lax
from jax.experimental import pallas as pl
from jax.experimental.pallas import tpu as pltpu
from jax.sharding import Mesh, PartitionSpec as P

SLOTS = 2
NAMES = ("yh", "x", "c", "yl", "z")
EXPERT = ("yh", "x", "c")
GROUP = ("yl", "z")
SWAP = [(0, 1), (1, 0)]
BF = jnp.bfloat16
F32 = jnp.float32

inv_root_two = 1.0 / math.sqrt(2.0)
inv_root_tau = 1.0 / math.sqrt(2.0 * math.pi)


def dot(a, b, ca, cb):
    return lax.dot_general(a, b, (((ca,), (cb,)), ((), ())), preferred_element_type=F32)


def params(limit=24):
    return pltpu.CompilerParams(vmem_limit_bytes=limit * 2**20)


def turn(core, z, step):
    return (core * 4 + z, core * 4 + (z + (step if core == 0 else -step)) % 4)


def up(value, name):
    with jax.named_scope(name + "_up"):
        return lax.ppermute(value, ("c", "z"), [turn(c, z, 1) for c in range(2) for z in range(4)])


def down(value, name):
    with jax.named_scope(name + "_down"):
        return lax.ppermute(value, ("c", "z"), [turn(c, z, -1) for c in range(2) for z in range(4)])


def across(value, name):
    with jax.named_scope(name + "_across"):
        return lax.ppermute(value, "yl", SWAP)


def one_hot_rows(rows, n_expert, resident):
    r = lax.broadcasted_iota(jnp.int32, (rows, rows), 0)
    k = lax.broadcasted_iota(jnp.int32, (rows, rows), 1)
    per = n_expert * SLOTS
    e, kind, source, s = r // (2 * per), r // per % 2, r % per // SLOTS, r % SLOTS
    wanted = ((source * 2 + kind) * resident + e) * SLOTS + s
    return (k == wanted).astype(F32).astype(BF)


def route_kernel(
    n_expert, tokens, slot_params, grad_out, rows, p_dispatch, p_combine, grad, sem
):
    copy = pltpu.make_async_copy(grad_out.at[0], grad, sem)
    copy.start()
    t = tokens[0]
    slots, feature = slot_params.shape
    logits = dot(slot_params[...], t, 1, 1)
    wide = jnp.exp(logits - jnp.max(logits, axis=1, keepdims=True))
    pd = wide / jnp.sum(wide, axis=1, keepdims=True)
    p_dispatch[...] = pd
    tall = jnp.exp(logits - jnp.max(logits, axis=0, keepdims=True))
    pc = tall / jnp.sum(tall, axis=0, keepdims=True)
    p_combine[...] = pc
    shape = (n_expert, slots // n_expert, feature)
    slot_in = dot(pd.astype(BF), t, 1, 0).reshape(shape)
    copy.wait()
    d_slot_out = dot(pc.astype(BF), grad[...], 1, 0).reshape(shape)
    both = jnp.concatenate([slot_in, d_slot_out], axis=1).astype(BF)
    rows[...] = both.reshape(rows.shape)


def route(tokens, slot_params, grad_out, n_expert):
    _, length, feature = tokens.shape
    slots = slot_params.shape[0]
    rows = jax.ShapeDtypeStruct((2 * slots, feature), BF)
    probs = jax.ShapeDtypeStruct((slots, length), F32)
    return pl.pallas_call(
        functools.partial(route_kernel, n_expert),
        in_specs=[
            pl.BlockSpec(memory_space=pltpu.VMEM),
            pl.BlockSpec(memory_space=pltpu.VMEM),
            pl.BlockSpec(memory_space=pl.ANY),
        ],
        out_shape=(rows, probs, probs),
        scratch_shapes=[pltpu.VMEM((length, feature), BF), pltpu.SemaphoreType.DMA],
        compiler_params=params(60),
        name="route",
    )(tokens, slot_params, grad_out)


def sort_kernel(n_expert, resident, rows, first, second):
    n = rows.shape[0]
    out = dot(one_hot_rows(n, n_expert, resident), rows[...], 1, 0).astype(BF)
    half = out.reshape(2, *first.shape)
    first[...] = half[0]
    second[...] = half[1]


def sort_rows(rows, n_expert, resident):
    n, feature = rows.shape
    half = jax.ShapeDtypeStruct((resident // 2, n // resident, feature), BF)
    return pl.pallas_call(
        functools.partial(sort_kernel, n_expert, resident),
        out_shape=(half, half),
        compiler_params=params(),
        name="sort_rows",
    )(rows)


def after(values, others):
    return lax.optimization_barrier((tuple(values), tuple(others)))[0]


def stage_kernel(w_in, w_out, near_in, near_out, sems):
    copies = [
        pltpu.make_async_copy(w_in, near_in, sems.at[0]),
        pltpu.make_async_copy(w_out, near_out, sems.at[1]),
    ]
    for copy in copies:
        copy.start()
    for copy in copies:
        copy.wait()


def stage(w_in, w_out):
    return pl.pallas_call(
        stage_kernel,
        in_specs=[pl.BlockSpec(memory_space=pltpu.HBM)] * 2,
        out_specs=[pl.BlockSpec(memory_space=pl.ANY)] * 2,
        out_shape=[jax.ShapeDtypeStruct(w.shape, w.dtype) for w in (w_in, w_out)],
        scratch_shapes=[pltpu.SemaphoreType.DMA((2,))],
        compiler_params=params(40),
        name="stage",
    )(w_in, w_out)


def gather(first, second, w_in, w_out):
    low1, high1, y1 = up(first, "first"), down(first, "first"), across(first, "first")
    low2, high2, y2 = up(second, "second"), down(second, "second"), across(second, "second")
    far1, far2 = up(low1, "first_on"), down(high2, "second_on")
    (y1,) = after((y1,), (high1,))
    y_low1, y_high1 = up(y1, "first_y"), down(y1, "first_y")
    weights = stage(*after((w_in, w_out), (y_low1,)))
    one = (first, low1, far1, high1, y1, y_low1, across(far1, "first_far"), y_high1)
    (y2,) = after((y2,), (far1,))
    y_low2, y_high2 = up(y2, "second_y"), down(y2, "second_y")
    (far2,) = after((far2,), weights)
    two = (second, low2, far2, high2, y2, y_low2, across(far2, "second_far"), y_high2)
    return one, two, weights


def assemble(refs, into):
    part = refs[0].shape[1] // 2
    for place, ref in enumerate(refs):
        for kind in range(2):
            into[kind, place * part : (place + 1) * part] = ref[0, kind * part : (kind + 1) * part]


def scatter_out(kind, total, refs):
    part = refs[0].shape[1] // 2
    for place, ref in enumerate(refs):
        ref[0, kind * part : (kind + 1) * part] = total[place * part : (place + 1) * part]


def expert_kernel(*refs):
    pieces, (w_in, w_out), (active, d_hidden) = refs[:8], refs[8:10], refs[10:12]
    partial, rows = refs[12:20], refs[20]
    assemble(pieces, rows)
    hidden = dot(w_in[0], rows[0], 1, 1)
    d_active = dot(w_out[0], rows[1], 1, 1)
    bell = 0.5 * (1.0 + lax.erf(hidden * inv_root_two))
    act = (hidden * bell).astype(BF)
    active[0] = act
    slope = bell + hidden * jnp.exp(-0.5 * hidden * hidden) * inv_root_tau
    dh = (d_active * slope).astype(BF)
    d_hidden[0] = dh
    scatter_out(0, dot(act, w_out[0], 0, 0).astype(BF), partial)
    scatter_out(1, dot(dh, w_in[0], 0, 0).astype(BF), partial)


def per_expert(*shape, base=0):
    return pl.BlockSpec((1, *shape), lambda e: (e + base, 0, 0))


def expert_call(pieces, w_in, w_out, base):
    _, hid, feature = w_in.shape
    count, block, _ = pieces[0].shape
    total = 4 * block
    work = count * hid * total * feature
    return pl.pallas_call(
        expert_kernel,
        grid=(count,),
        in_specs=[per_expert(block, feature)] * 8 + [per_expert(hid, feature, base=base)] * 2,
        out_specs=[per_expert(hid, total)] * 2 + [per_expert(block, feature)] * 8,
        out_shape=[jax.ShapeDtypeStruct((count, hid, total), BF)] * 2
        + [jax.ShapeDtypeStruct((count, block, feature), BF)] * 8,
        scratch_shapes=[pltpu.VMEM((2, total, feature), BF)],
        compiler_params=params(24),
        cost_estimate=pl.CostEstimate(flops=8 * work, bytes_accessed=12 * 2**20, transcendentals=0),
        name="expert",
    )(*pieces, w_in, w_out)


def weights_kernel(half, *refs):
    one, two = refs[:10], refs[10:20]
    grad_w_out, grad_w_in, rows = refs[20:]

    def work(pieces, active, d_hidden):
        assemble(pieces, rows)
        grad_w_out[0] = dot(active[0], rows[1], 1, 0).astype(BF)
        grad_w_in[0] = dot(d_hidden[0], rows[0], 1, 0).astype(BF)

    @pl.when(pl.program_id(0) < half)
    def _():
        work(one[:8], *one[8:])

    @pl.when(pl.program_id(0) >= half)
    def _():
        work(two[:8], *two[8:])


def weight_grads(one, two):
    half, hid, total = one[8].shape
    block, feature = one[0].shape[1:]

    def first(*shape):
        return pl.BlockSpec((1, *shape), lambda e: (jnp.minimum(e, half - 1), 0, 0))

    def second(*shape):
        return pl.BlockSpec((1, *shape), lambda e: (jnp.maximum(e - half, 0), 0, 0))

    in_specs = []
    for spec in (first, second):
        in_specs += [spec(block, feature)] * 8 + [spec(hid, total)] * 2
    out = jax.ShapeDtypeStruct((2 * half, hid, feature), BF)
    work = 2 * half * hid * total * feature
    return pl.pallas_call(
        functools.partial(weights_kernel, half),
        grid=(2 * half,),
        in_specs=in_specs,
        out_specs=[per_expert(hid, feature)] * 2,
        out_shape=[out, out],
        scratch_shapes=[pltpu.VMEM((2, total, feature), BF)],
        compiler_params=params(60),
        cost_estimate=pl.CostEstimate(flops=4 * work, bytes_accessed=20 * 2**20, transcendentals=0),
        name="weight_grads",
    )(*one, *two)


def add(*values):
    return sum(v.astype(F32) for v in values).astype(BF)


def reduce(parts, far_way, name, wait=False):
    own, low, far, high, y, y_low, y_far, y_high = parts
    w = across(y_far, name + "_far")
    v_up, v_down = up(y_high, name + "_y"), down(y_low, name + "_y")
    near, last, other_way = (low, high, down) if far_way is up else (high, low, up)
    h = far_way(add(far, w), name + "_on")
    if wait:
        (near,) = after((near,), (h,))
    direct = other_way(near, name)
    chain = far_way(add(last, h), name)
    if not wait:
        y, v_up, v_down = after((y, v_up, v_down), (direct,))
    return own, direct, chain, across(add(y, v_up, v_down), name)


def unsort_kernel(n_expert, n_first, *refs):
    out = refs[-1]
    half, block, feature = refs[0].shape
    n = 2 * half * block
    first = sum(ref[...].astype(F32) for ref in refs[:n_first])
    second = sum(ref[...].astype(F32) for ref in refs[n_first:-1])
    total = jnp.concatenate([first, second], axis=0).reshape(n, feature).astype(BF)
    out[...] = dot(one_hot_rows(n, n_expert, 2 * half), total, 0, 0).astype(BF)


def unsort_rows(first, second, n_expert):
    half, block, feature = first[0].shape
    return pl.pallas_call(
        functools.partial(unsort_kernel, n_expert, len(first)),
        out_shape=jax.ShapeDtypeStruct((2 * half * block, feature), BF),
        compiler_params=params(),
        name="unsort_rows",
    )(*first, *second)


def exchange(rows):
    return lax.all_to_all(rows, EXPERT, split_axis=0, concat_axis=0, tiled=True)


def logits_kernel(n_expert, tokens, grad_out, back, p_dispatch, p_combine, d_logits, local, d_slot):
    t = tokens[0]
    n, feature = back.shape
    wide = back[...].astype(F32).reshape(n_expert, n // n_expert, feature)
    split = n // n_expert // 2
    slot_out = wide[:, :split].reshape(n // 2, feature).astype(BF)
    d_slot_in = wide[:, split:].reshape(n // 2, feature).astype(BF)
    d_slot[...] = d_slot_in
    d_combine = dot(slot_out, grad_out[0], 1, 1)
    d_dispatch = dot(d_slot_in, t, 1, 1)
    pd, pc = p_dispatch[...], p_combine[...]
    grad = pd * (d_dispatch - jnp.sum(pd * d_dispatch, axis=1, keepdims=True)) + pc * (
        d_combine - jnp.sum(pc * d_combine, axis=0, keepdims=True)
    )
    dl = grad.astype(BF)
    d_logits[...] = dl
    local[...] = dot(dl, t, 1, 0).reshape(local.shape)


def logits_back(tokens, grad_out, back, p_dispatch, p_combine, n_expert):
    slots = p_dispatch.shape[0]
    feature = back.shape[1]
    return pl.pallas_call(
        functools.partial(logits_kernel, n_expert),
        out_shape=(
            jax.ShapeDtypeStruct(p_dispatch.shape, BF),
            jax.ShapeDtypeStruct((slots, 1, feature), F32),
            jax.ShapeDtypeStruct((slots, feature), BF),
        ),
        compiler_params=params(),
        name="logits_back",
    )(tokens, grad_out, back, p_dispatch, p_combine)


def tokens_kernel(p_dispatch, d_slot_in, d_logits, slot_params, grad_tokens):
    first = dot(p_dispatch[...].astype(BF), d_slot_in[...], 0, 0)
    second = dot(d_logits[...], slot_params[...], 0, 0)
    grad_tokens[0] = (first + second).astype(BF)


def tokens_back(p_dispatch, d_slot_in, d_logits, slot_params):
    slots, length = p_dispatch.shape
    feature = slot_params.shape[1]
    return pl.pallas_call(
        tokens_kernel,
        out_shape=jax.ShapeDtypeStruct((1, length, feature), BF),
        compiler_params=params(),
        name="tokens_back",
    )(p_dispatch, d_slot_in, d_logits, slot_params)


def sum_kernel(terms, copies):
    total = jnp.sum(terms[...], axis=0, keepdims=True)
    copies[...] = jnp.broadcast_to(total, copies.shape)


def sum_over_all(value):
    slots, _, feature = value.shape
    terms = lax.all_to_all(value, NAMES, split_axis=0, concat_axis=0, tiled=True)
    copies = pl.pallas_call(
        sum_kernel,
        out_shape=jax.ShapeDtypeStruct(value.shape, F32),
        compiler_params=params(),
        name="sum_terms",
    )(terms)
    total = lax.all_to_all(copies, NAMES, split_axis=0, concat_axis=0, tiled=True)
    return total.reshape(slots, feature)


def split(outputs):
    return outputs[:2], outputs[2:]


def per_device(tokens, slot_params, expert_in, expert_out, grad_out):
    n_expert = lax.axis_size(EXPERT)
    resident = expert_in.shape[0]
    outgoing, p_dispatch, p_combine = route(tokens, slot_params, grad_out, n_expert)
    first, second = sort_rows(exchange(outgoing), n_expert, resident)
    one, two, weights = gather(first, second, expert_in, expert_out)
    kept_one, partial_one = split(expert_call(one, *weights, 0))
    sums_one = reduce(partial_one, up, "sum_first")
    kept_two, partial_two = split(expert_call(two, *weights, resident // 2))
    sums_two = reduce(partial_two, down, "sum_second", True)
    grad_w_out, grad_w_in = weight_grads((*one, *kept_one), (*two, *kept_two))
    back = exchange(unsort_rows(sums_one, sums_two, n_expert))
    d_logits, local_params, d_slot_in = logits_back(
        tokens, grad_out, back, p_dispatch, p_combine, n_expert
    )
    grad_params = sum_over_all(local_params)
    grad_tokens = tokens_back(p_dispatch, d_slot_in, d_logits, slot_params)
    return (grad_tokens, grad_params, grad_w_in, grad_w_out)


def solution(mesh):
    parts = Mesh(mesh.devices.reshape(2, 4, 2, 2, 4), NAMES)
    image = P(NAMES, None, None)
    weight = P(EXPERT, GROUP, None)
    return jax.shard_map(
        per_device,
        mesh=parts,
        in_specs=(image, P(), weight, weight, image),
        out_specs=(image, P(), weight, weight),
        check_vma=False,
    )
```
